32 devices in a mesh: row: 4 (over z), col: 8 (over y, x, core).
Axes of the slice: x: 2, y: 2, z: 4, core: 2. Of those that a mesh axis runs over, the one named last changes fastest.
Arguments:
- a_blocks: bfloat16 [256, 8, 4, 4096], P('row', 'col'), may hold values from -0.1875 to 0.1875
- a_index: int32 [256, 8, 4], P('row', 'col'), may hold values from 0 to 31, as said below
- p_blocks: bfloat16 [32, 8, 4, 4096], P('row', 'col'), may hold values from -2 to 2
- p_index: int32 [32, 8, 4], P('row', 'col'), may hold values from 0 to 31, as said below
- ap_index: int32 [256, 8], P('row'), may hold values from 0 to 31, as said below
- coarse_index: int32 [32, 8], replicated, may hold values from 0 to 31, as said below
Outputs:
- ap_out: bfloat16 [32, 8, 8, 4096], P('row', 'col')
- coarse_out: float32 [32, 8, 4096], P(('row', 'col'))
The draws below stay inside these ranges and needn't reach their ends.
Inputs may be any that keep to these rules, and one draw needn't show every extreme that they name: `a_index`: within one (i, c) the 4 entries are distinct. `p_index`: within one row the 4 entries are distinct. `ap_index`: within one row the 8 entries are distinct. `coarse_index`: within one row the 8 entries are distinct.
All inputs are finite; a program needn't handle non-finite values.
Results may differ from the reference program's by a relative error of at most 0.0029.
Values may be sent and summed in bfloat16 or wider, within the bound.
A program may use at most 320 MiB of HBM per device.

```python
import jax
import jax.numpy as jnp
from jax import lax

B = 64
KA = 4
KP = 4
KAP = 8
KC = 8
NB = 256
NQ = 32
NCB = 32
SPAN = 11
OFFLO = 5
N_COL = 8


def hub_table(key):
    return jax.random.randint(jax.random.fold_in(key, 11), (NCB,), 0, NQ)


def aggregate_order(key):
    return jax.random.permutation(jax.random.fold_in(key, 13), NCB).astype(jnp.int32)


def distinct_pick(key, lead, width, keep):
    scores = jax.random.randint(key, lead + (width,), 0, 2 ** 20)
    scores = scores * width + jnp.arange(width, dtype=jnp.int32)
    order = jnp.argsort(scores, axis=-1, stable=True).astype(jnp.int32)
    return order[..., :keep]


def draw_a_index(key, part):
    hubs = hub_table(key)
    fine = jnp.arange(NB, dtype=jnp.int32)
    base = hubs[fine // 8]
    delta = distinct_pick(jax.random.fold_in(key, 21), (NB, N_COL), 7, KA) - 3
    return ((base[:, None, None] + delta) % NQ).astype(jnp.int32)


def draw_p_index(key, part):
    relabel = aggregate_order(key)
    fine = jnp.arange(NQ, dtype=jnp.int32)[:, None] * N_COL + jnp.arange(N_COL, dtype=jnp.int32)[None, :]
    delta = distinct_pick(jax.random.fold_in(key, 31), (NQ, N_COL), 5, KP) - 2
    geometric = ((fine[:, :, None] // 8 + delta) % NCB).astype(jnp.int32)
    return relabel[geometric].astype(jnp.int32)


def draw_ap_index(key, part):
    hubs = hub_table(key)
    relabel = aggregate_order(key)
    fine = jnp.arange(NB, dtype=jnp.int32)
    base = hubs[fine // 8] * N_COL // 8 - OFFLO
    offset = distinct_pick(jax.random.fold_in(key, 41), (NB,), SPAN, KAP)
    geometric = ((base[:, None] + offset) % NCB).astype(jnp.int32)
    return relabel[geometric].astype(jnp.int32)


def draw_coarse_index(key, part):
    hubs = hub_table(key)
    relabel = aggregate_order(key)
    base = hubs * N_COL // 8 - OFFLO
    offset = distinct_pick(jax.random.fold_in(key, 51), (NCB,), SPAN, KC)
    geometric = ((base[:, None] + offset) % NCB).astype(jnp.int32)
    values = relabel[geometric].astype(jnp.int32)
    result = jnp.zeros((NCB, KC), jnp.int32).at[relabel].set(values)
    return result.astype(jnp.int32)


def steps_of(own_key, dims, shards, smallest, largest):
    def one(position, parts):
        steps = jax.random.uniform(jax.random.fold_in(jax.random.fold_in(own_key, 6), position), (parts,), jnp.float32, smallest / len(shards), largest / len(shards))
        return jnp.repeat(jnp.exp(steps), dims[position] // parts).reshape((-1,) + (1,) * (len(dims) - position - 1))

    level = one(*shards[0])
    for cut in shards[1:]:
        level = level * one(*cut)
    return level


def normal_values(stream_key, extent, spread, most, cuts=(), kind=jnp.bfloat16):
    level = steps_of(stream_key, extent, cuts, -0.22, 0.18) if cuts else 1.0
    array = jax.random.normal(stream_key, extent, jnp.float32) * spread * level
    return jnp.minimum(jnp.maximum(array, -most), most).astype(kind)


def setup_inputs(seed: int = 0) -> dict:
    keys = jax.random.split(jax.random.key(seed), 7)
    a_blocks = normal_values(keys[0], (NB, N_COL, KA, B * B), (B * KA * N_COL // 2) ** -0.5, 0.1875, ((0, 4), (1, 8)))
    a_index = draw_a_index(jax.random.fold_in(keys[6], 71), 0)
    p_blocks = normal_values(keys[2], (NQ, N_COL, KP, B * B), 0.35, 2.0, ((0, 4), (1, 8)))
    p_index = draw_p_index(jax.random.fold_in(keys[6], 71), 0)
    ap_index = draw_ap_index(jax.random.fold_in(keys[6], 71), 0)
    coarse_index = draw_coarse_index(jax.random.fold_in(keys[6], 71), 0)
    return dict(a_blocks=a_blocks, a_index=a_index, p_blocks=p_blocks, p_index=p_index, ap_index=ap_index, coarse_index=coarse_index)


def reference(a_blocks, a_index, p_blocks, p_index, ap_index, coarse_index):
    hp = lax.Precision.HIGHEST
    prolong = p_blocks.reshape(NB, KP, B, B)
    prolong_cols = p_index.reshape(NB, KP)
    group_pos = jnp.arange(N_COL, dtype=jnp.int32)[None, :, None]
    fine_cols = (a_index * N_COL + group_pos).astype(jnp.int32).reshape(NB, N_COL * KA)
    jac_rows = a_blocks.reshape(NB, N_COL * KA, B, B)

    def one_row(packed):
        blocks, fine_k, slots = packed
        picked = jnp.take(prolong, fine_k, axis=0).astype(jnp.float32)
        picked_cols = jnp.take(prolong_cols, fine_k, axis=0)
        product = jnp.einsum('nax,nmxb->nmab', blocks.astype(jnp.float32), picked, precision=hp)
        match = (picked_cols[:, :, None] == slots[None, None, :]).astype(jnp.float32)
        return jnp.einsum('nms,nmab->sab', match, product, precision=hp)

    ap_full = lax.map(one_row, (jac_rows, fine_cols, ap_index))
    ap_low = ap_full.astype(jnp.bfloat16)

    step_rows = 8
    prolong_steps = prolong.reshape(NB // step_rows, step_rows, KP, B, B)
    pcol_steps = prolong_cols.reshape(NB // step_rows, step_rows, KP)
    ap_steps = ap_low.reshape(NB // step_rows, step_rows, KAP, B, B)
    slot_steps = ap_index.reshape(NB // step_rows, step_rows, KAP)

    def add_block(total, packed):
        pro_blk, pcol_blk, ap_blk, slot_blk = packed
        terms = jnp.einsum('umxa,usxb->umsab', pro_blk.astype(jnp.float32), ap_blk.astype(jnp.float32), precision=hp)
        targets = jnp.take(coarse_index, pcol_blk, axis=0)
        equal = targets[:, :, None, :] == slot_blk[:, None, :, None]
        where_slot = jnp.sum(jnp.where(equal, lax.broadcasted_iota(jnp.int32, equal.shape, 3), 0), axis=3).astype(jnp.int32)
        found = jnp.any(equal, axis=3)
        flat = jnp.where(found, pcol_blk[:, :, None] * KC + where_slot, NCB * KC).astype(jnp.int32).reshape(-1)
        total = total.at[flat].add(terms.reshape(-1, B * B), mode="drop")
        return total, None

    start = jnp.zeros((NCB * KC, B * B), jnp.float32)
    coarse_total, unused = lax.scan(add_block, start, (prolong_steps, pcol_steps, ap_steps, slot_steps))
    return ap_low.reshape(NQ, N_COL, KAP, B * B), coarse_total.reshape(NCB, KC, B * B)
```

```python
import functools

import jax
import jax.numpy as jnp
from jax import lax
from jax.experimental import pallas as pl
from jax.experimental.pallas import tpu as pltpu
from jax.sharding import PartitionSpec as P

MESH = pl.DeviceIdType.MESH
F32 = jnp.float32
BF16 = jnp.bfloat16


def left_mask(half):
    return lax.broadcasted_iota(jnp.int32, (half, 4 * half), 1) < 2 * half


def swap(x):
    return pltpu.roll(x, x.shape[1] // 2, 1)


def halves(x, left):
    other = swap(x)
    zero = jnp.zeros_like(x)
    in_left = jnp.concatenate([jnp.where(left, x, zero), jnp.where(left, other, zero)], axis=0)
    in_right = jnp.concatenate([jnp.where(left, zero, other), jnp.where(left, zero, x)], axis=0)
    return in_left.astype(BF16), in_right.astype(BF16)


def interleave(tile, left):
    half = left.shape[0]
    top, bottom = tile[:half], tile[half:]
    return jnp.where(left, top, swap(bottom)), jnp.where(left, swap(top), bottom)


def gather_tiles(in_left, in_right, picks):
    return jnp.concatenate(
        [in_left[picks[n]] + in_right[picks[n + 1]] for n in range(0, len(picks), 2)], axis=1
    )


def kernel(
    sizes, a_ref, pg_ref, pown_ref, order_ref, aidx_ref, pidx_ref, sidx_ref,
    ap_out, coarse_out,
    pl_l, pl_r, pt_l, pt_r, apl, apr,
    s1a, r1a, s2a, r2a, acc_a, s1b, r1b, s2b, r2b, acc_b, r3,
    s1a_send, s1a_recv, s2a_send, s2a_recv, s1b_send, s1b_recv, s2b_send, s2b_recv, s3_send, s3_recv,
):
    rows, cols, own, ka, kp, kap, kc, per, groups = sizes
    chips = cols // 2
    half = pg_ref.shape[1]
    width = 2 * half
    left = left_mask(half)
    row, col = lax.axis_index("row"), lax.axis_index("col")
    core = lax.rem(col, 2)
    chip = col // 2
    partner = chip * 2 + 1 - core

    barrier = pltpu.get_barrier_semaphore()
    pl.semaphore_signal(barrier, inc=1, device_id=(row, partner), device_id_type=MESH)
    for d in range(1, chips):
        there = lax.rem(chip + d, chips) * 2 + core
        pl.semaphore_signal(barrier, inc=1, device_id=(row, there), device_id_type=MESH)
    for d in range(1, rows):
        pl.semaphore_signal(
            barrier, inc=1, device_id=(lax.rem(row + d, rows), col), device_id_type=MESH
        )

    def spread(n, carry):
        in_left, in_right = halves(pg_ref[n].astype(F32), left)
        pl_l[n] = in_left
        pl_r[n] = in_right
        return carry

    lax.fori_loop(0, groups, spread, 0, unroll=4)
    pl_l[groups] = jnp.zeros(pl_l.shape[1:], BF16)
    pl_r[groups] = jnp.zeros(pl_r.shape[1:], BF16)
    pl.semaphore_wait(barrier, chips + rows - 1)

    def product_row(to, u):
        i = u * cols + to
        lhs = []
        for e in range(0, ka, 2):
            x0, x1 = a_ref[i, e].astype(F32), a_ref[i, e + 1].astype(F32)
            top = jnp.where(left, x0, swap(x1))
            bottom = jnp.where(left, swap(x0), x1)
            lhs.append(jnp.concatenate([top, bottom], axis=0).astype(BF16))
        base = i * (ka * kap)
        rhs = [
            gather_tiles(pl_l, pl_r, [aidx_ref[base + e * kap + s] for s in range(kap)])
            for e in range(ka)
        ]
        return jnp.dot(
            jnp.concatenate(lhs, axis=1), jnp.concatenate(rhs, axis=0), preferred_element_type=F32
        )

    def coarse_row(to, n):
        j = ((n // per) * cols + to) * per + lax.rem(n, per)
        lhs = gather_tiles(pt_l, pt_r, [pidx_ref[j * own + u] for u in range(own)])
        rhs = [
            gather_tiles(apl, apr, [sidx_ref[(j * own + u) * kc + t] for t in range(kc)])
            for u in range(own)
        ]
        return jnp.dot(lhs, jnp.concatenate(rhs, axis=0), preferred_element_type=F32)

    def reduce_plane(compute, count, s1, r1, s2, r2, acc, sems, before_wait):
        s1_send, s1_recv, s2_send, s2_recv = sems
        order = list(range(1, chips)) + [0]
        first, second = [], []

        def give(n):
            d = order[n]
            to = lax.rem(chip + d, chips) * 2 + 1 - core
            slot = n % s1.shape[0]
            if n >= s1.shape[0]:
                first[n - s1.shape[0]].wait_send()

            def body(k, carry):
                s1[slot, k] = compute(to, k)
                return carry

            lax.fori_loop(0, count, body, 0)
            copy = pltpu.make_async_remote_copy(
                src_ref=s1.at[slot], dst_ref=r1.at[n], send_sem=s1_send.at[n], recv_sem=s1_recv.at[n],
                device_id=(row, partner), device_id_type=MESH,
            )
            copy.start()
            first.append(copy)

        def finish(n):
            d = order[n]
            to = lax.rem(chip + d, chips) * 2 + core
            slot = n % s2.shape[0]
            first[n].wait_recv()
            if d and n >= s2.shape[0]:
                second[n - s2.shape[0]].wait_send()

            def body(k, carry):
                value = compute(to, k) + r1[n, k]
                if d:
                    s2[slot, k] = value.astype(s2.dtype)
                else:
                    acc[k] = value
                return carry

            lax.fori_loop(0, count, body, 0)
            if d:
                copy = pltpu.make_async_remote_copy(
                    src_ref=s2.at[slot], dst_ref=r2.at[n], send_sem=s2_send.at[n], recv_sem=s2_recv.at[n],
                    device_id=(row, to), device_id_type=MESH,
                )
                copy.start()
                second.append(copy)

        for n in range(chips):
            give(n)
            if n:
                finish(n - 1)
        finish(chips - 1)
        before_wait()
        for n in range(max(0, chips - s1.shape[0]), chips):
            first[n].wait_send()
        for copy in second:
            copy.wait_recv()
        for n in range(max(0, chips - 1 - s2.shape[0]), chips - 1):
            second[n].wait_send()

        def total(k):
            value = acc[k]
            for n in range(chips - 1):
                value = value + r2[n, k].astype(F32)
            return value

        return total

    def turn_prolongator():
        order_mat = order_ref[...]

        def body(n, carry):
            block = halves(pown_ref[n].astype(F32), left)[0]
            zero = jnp.zeros_like(block)
            contract = (((1,), (1,)), ((), ()))
            pt_l[n] = lax.dot_general(
                order_mat, jnp.concatenate([block, zero], axis=0), contract, preferred_element_type=F32
            ).astype(BF16)
            pt_r[n] = lax.dot_general(
                order_mat, jnp.concatenate([zero, block], axis=0), contract, preferred_element_type=F32
            ).astype(BF16)
            return carry

        lax.fori_loop(0, own * kp, body, 0, unroll=2)
        pt_l[own * kp] = jnp.zeros(pt_l.shape[1:], BF16)
        pt_r[own * kp] = jnp.zeros(pt_r.shape[1:], BF16)

    total = reduce_plane(
        product_row, own, s1a, r1a, s2a, r2a, acc_a, (s1a_send, s1a_recv, s2a_send, s2a_recv), turn_prolongator
    )

    def keep(u, carry):
        value = total(u).astype(BF16).astype(F32)
        for s in range(0, kap, 2):
            tile = value[:, s * width : (s + 2) * width]
            x0, x1 = interleave(tile, left)
            ap_out[u, s] = x0.astype(BF16)
            ap_out[u, s + 1] = x1.astype(BF16)
            for n, x in ((s, x0), (s + 1, x1)):
                in_left, in_right = halves(x, left)
                apl[u * kap + n] = in_left
                apr[u * kap + n] = in_right
        return carry

    lax.fori_loop(0, own, keep, 0)
    apl[own * kap] = jnp.zeros(apl.shape[1:], BF16)
    apr[own * kap] = jnp.zeros(apr.shape[1:], BF16)

    coarse_total = reduce_plane(
        coarse_row, rows * per, s1b, r1b, s2b, r2b, acc_b, (s1b_send, s1b_recv, s2b_send, s2b_recv), lambda: None
    )

    def gather_sum(n, carry):
        acc_b[n] = coarse_total(n)
        return carry

    lax.fori_loop(0, rows * per, gather_sum, 0)
    third = []
    for d in range(1, rows):
        to = lax.rem(row + d, rows)
        copy = pltpu.make_async_remote_copy(
            src_ref=acc_b.at[pl.ds(to * per, per)], dst_ref=r3.at[d - 1],
            send_sem=s3_send.at[d - 1], recv_sem=s3_recv.at[d - 1],
            device_id=(to, col), device_id_type=MESH,
        )
        copy.start()
        third.append(copy)
    for copy in third:
        copy.wait()
    for q in range(per):
        value = acc_b[row * per + q]
        for d in range(1, rows):
            value = value + r3[d - 1, q]
        for t in range(0, kc, 2):
            x0, x1 = interleave(value[:, t * width : (t + 2) * width], left)
            coarse_out[q, t] = x0
            coarse_out[q, t + 1] = x1


def shards(a_blocks, a_index, p_blocks, p_index, ap_index, coarse_index):
    rows, cols = lax.axis_size("row"), lax.axis_size("col")
    count, _, ka, flat = a_blocks.shape
    own, _, kp, _ = p_blocks.shape
    kap = ap_index.shape[1]
    coarse, kc = coarse_index.shape
    per = coarse // (rows * cols)
    width = int(round(flat ** 0.5))
    half = width // 2
    lanes = 2 * width

    a2 = a_blocks.reshape(count, ka, half, lanes)
    p2 = p_blocks.reshape(own * kp, half, lanes)
    p_nat = p_blocks.reshape(own * kp, 2, half, width).transpose(0, 2, 1, 3).reshape(own * kp, half, lanes)
    group = lax.all_gather(p_nat, "row", axis=0, tiled=True)
    group_cols = lax.all_gather(p_index[:, 0], "row", axis=0, tiled=True)
    groups = group.shape[0]

    fine = a_index[:, 0]
    hot = fine[:, :, None, None] == lax.broadcasted_iota(jnp.int32, (1, 1, group_cols.shape[0], 1), 2)
    picked = jnp.sum(jnp.where(hot, group_cols[None, None], 0), axis=2)
    same = picked[:, :, :, None] == ap_index[:, None, None, :]
    place = fine[:, :, None, None] * kp + lax.broadcasted_iota(jnp.int32, (1, 1, kp, 1), 2)
    a_pick = jnp.where(jnp.any(same, axis=2), jnp.sum(jnp.where(same, place, 0), axis=2), groups)

    mine = p_index[:, 0]
    slots = lax.dynamic_index_in_dim(ap_index.reshape(own, cols, kap), lax.axis_index("col"), 1, keepdims=False)
    which = jnp.arange(own * kp, dtype=jnp.int32).reshape(own, kp)
    hit = mine[None] == jnp.arange(coarse, dtype=jnp.int32)[:, None, None]
    p_pick = jnp.where(jnp.any(hit, axis=2), jnp.sum(jnp.where(hit, which[None], 0), axis=2), own * kp)
    spot = jnp.arange(own * kap, dtype=jnp.int32).reshape(own, kap)
    match = coarse_index[:, None, :, None] == slots[None, :, None, :]
    s_pick = jnp.where(
        jnp.any(match, axis=3), jnp.sum(jnp.where(match, spot[None, :, None, :], 0), axis=3), own * kap
    )

    into = jnp.arange(width, dtype=jnp.int32)
    source = (into % half) * 2 + into // half
    order_mat = (source[:, None] == jnp.arange(lanes, dtype=jnp.int32)[None, :]).astype(BF16)

    chips = cols // 2
    others = max(chips - 1, 1)
    slots2 = min(others, 3)
    wide = kap * width
    wide_c = kc * width
    vmem = pl.BlockSpec(memory_space=pltpu.VMEM)
    smem = pl.BlockSpec(memory_space=pltpu.SMEM)
    dma = pltpu.SemaphoreType.DMA
    n_coarse = rows * per
    ap, coarse_out = pl.pallas_call(
        functools.partial(kernel, (rows, cols, own, ka, kp, kap, kc, per, groups)),
        out_shape=(
            jax.ShapeDtypeStruct((own, kap, half, lanes), BF16),
            jax.ShapeDtypeStruct((per, kc, half, lanes), F32),
        ),
        in_specs=[vmem, vmem, vmem, vmem, smem, smem, smem],
        out_specs=(vmem, vmem),
        scratch_shapes=[
            pltpu.VMEM((groups + 1, width, lanes), BF16),
            pltpu.VMEM((groups + 1, width, lanes), BF16),
            pltpu.VMEM((own * kp + 1, width, lanes), BF16),
            pltpu.VMEM((own * kp + 1, width, lanes), BF16),
            pltpu.VMEM((own * kap + 1, width, lanes), BF16),
            pltpu.VMEM((own * kap + 1, width, lanes), BF16),
            pltpu.VMEM((2, own, width, wide), F32),
            pltpu.VMEM((chips, own, width, wide), F32),
            pltpu.VMEM((slots2, own, width, wide), BF16),
            pltpu.VMEM((others, own, width, wide), BF16),
            pltpu.VMEM((own, width, wide), F32),
            pltpu.VMEM((2, n_coarse, width, wide_c), F32),
            pltpu.VMEM((chips, n_coarse, width, wide_c), F32),
            pltpu.VMEM((slots2, n_coarse, width, wide_c), F32),
            pltpu.VMEM((others, n_coarse, width, wide_c), F32),
            pltpu.VMEM((n_coarse, width, wide_c), F32),
            pltpu.VMEM((max(rows - 1, 1), per, width, wide_c), F32),
            dma((chips,)), dma((chips,)), dma((others,)), dma((others,)),
            dma((chips,)), dma((chips,)), dma((others,)), dma((others,)),
            dma((max(rows - 1, 1),)), dma((max(rows - 1, 1),)),
        ],
        compiler_params=pltpu.CompilerParams(
            collective_id=0, has_side_effects=True, vmem_limit_bytes=60 * 1024 * 1024
        ),
    )(a2, group, p2, order_mat, a_pick.reshape(-1), p_pick.reshape(-1), s_pick.reshape(-1))
    return ap.reshape(own, 1, kap, flat), coarse_out.reshape(per, kc, flat)


def solution(mesh):
    placed = (
        P("row", "col", None, None),
        P("row", "col", None),
        P("row", "col", None, None),
        P("row", "col", None),
        P("row", None),
        P(),
    )
    return jax.shard_map(
        shards,
        mesh=mesh,
        in_specs=placed,
        out_specs=(P("row", "col", None, None), P(("row", "col"), None, None)),
        check_vma=False,
    )
```

```python
import functools

import jax
import jax.numpy as jnp
import numpy as np
from jax import lax
from jax.experimental import pallas as pl
from jax.experimental.pallas import tpu as pltpu
from jax.sharding import PartitionSpec as P

MESH = pl.DeviceIdType.MESH
F32 = jnp.float32
BF16 = jnp.bfloat16
LINK = jnp.int16
TOP = 32766.0


def left_mask(half):
    return lax.broadcasted_iota(jnp.int32, (half, 4 * half), 1) < 2 * half


def swap(x):
    return pltpu.roll(x, x.shape[1] // 2, 1)


def halves(x, left):
    other = swap(x)
    zero = jnp.zeros_like(x)
    in_left = jnp.concatenate([jnp.where(left, x, zero), jnp.where(left, other, zero)], axis=0)
    in_right = jnp.concatenate([jnp.where(left, zero, other), jnp.where(left, zero, x)], axis=0)
    return in_left.astype(BF16), in_right.astype(BF16)


def interleave(tile, left):
    half = left.shape[0]
    top, bottom = tile[:half], tile[half:]
    return jnp.where(left, top, swap(bottom)), jnp.where(left, swap(top), bottom)


def pack(value):
    most = jnp.maximum(jnp.max(jnp.abs(value), axis=0, keepdims=True), 1e-30)
    return jnp.round(value * (TOP / most)).astype(jnp.int32).astype(LINK), most * (1.0 / TOP)


def unpack(value, scale):
    return value.astype(jnp.int32).astype(F32) * scale


def gather_tiles(in_left, in_right, picks):
    return jnp.concatenate(
        [in_left[picks[n]] + in_right[picks[n + 1]] for n in range(0, len(picks), 2)], axis=1
    )


def turn_prolongator(left, pown_ref, order_ref, pt_l, pt_r, mine):
    order_mat = order_ref[...]
    contract = (((1,), (1,)), ((), ()))

    def body(n, carry):
        block = halves(pown_ref[n].astype(F32), left)[0]
        zero = jnp.zeros_like(block)
        for ref, pair in ((pt_l, [block, zero]), (pt_r, [zero, block])):
            ref[n] = lax.dot_general(
                order_mat, jnp.concatenate(pair, axis=0), contract, preferred_element_type=F32
            ).astype(BF16)
        return carry

    lax.fori_loop(0, mine, body, 0, unroll=2)
    pt_l[mine] = jnp.zeros(pt_l.shape[1:], BF16)
    pt_r[mine] = jnp.zeros(pt_r.shape[1:], BF16)


def kernel(
    sizes, a_ref, pnat_ref, pown_ref, order_ref, table_ref, fine_ref, kept_ref, pidx_ref, sidx_ref,
    ap_out, coarse_out,
    pg, tables, places, pl_l, pl_r, pt_l, pt_r, apl, apr,
    s1a, r1a, s2a, r2a, s1a_c, r1a_c, s2a_c, r2a_c, acc_a,
    s1b, r1b, s2b, r2b, s1b_c, r1b_c, s2b_c, r2b_c, acc_b, mine_b, s3, r3, s3_c, r3_c,
    up_send, up_recv, down_send, down_recv, table_send, table_recv, place_sem,
    s1a_send, s1a_recv, s2a_send, s2a_recv, s1b_send, s1b_recv, s2b_send, s2b_recv, s3_send, s3_recv,
):
    rows, cols, own, ka, kp, kap, kc, per, groups = sizes
    chips = cols // 2
    half = pnat_ref.shape[1]
    width = 2 * half
    left = left_mask(half)
    row, col = lax.axis_index("row"), lax.axis_index("col")
    core = lax.rem(col, 2)
    chip = col // 2
    partner = chip * 2 + 1 - core

    barrier = pltpu.get_barrier_semaphore()
    pl.semaphore_signal(barrier, inc=1, device_id=(row, partner), device_id_type=MESH)
    for d in range(1, chips):
        there = lax.rem(chip + d, chips) * 2 + core
        pl.semaphore_signal(barrier, inc=1, device_id=(row, there), device_id_type=MESH)
    for d in range(1, rows):
        pl.semaphore_signal(
            barrier, inc=1, device_id=(lax.rem(row + d, rows), col), device_id_type=MESH
        )

    mine = own * kp
    pl_l[groups] = jnp.zeros(pl_l.shape[1:], BF16)
    pl_r[groups] = jnp.zeros(pl_r.shape[1:], BF16)
    here = pl.ds(pl.multiple_of(row * own, own), own)
    tables[here, :] = table_ref[...]
    pl.semaphore_wait(barrier, chips + rows - 1)

    def up(h):
        shard = row - h
        return (shard >= 0) & (row + 1 < rows), pltpu.make_async_remote_copy(
            src_ref=pg.at[shard] if h else pnat_ref, dst_ref=pg.at[shard],
            send_sem=up_send.at[h], recv_sem=up_recv.at[h],
            device_id=(row + 1, col), device_id_type=MESH,
        )

    def down(h):
        shard = row + h
        return (shard < rows) & (row > 0), pltpu.make_async_remote_copy(
            src_ref=pg.at[shard] if h else pnat_ref, dst_ref=pg.at[shard],
            send_sem=down_send.at[h], recv_sem=down_recv.at[h],
            device_id=(row - 1, col), device_id_type=MESH,
        )

    def start(ready, copy):
        @pl.when(ready)
        def _():
            copy.start()

    def done_send(ready, copy):
        @pl.when(ready)
        def _():
            copy.wait_send()

    def spread(source, shard):
        def body(n, carry):
            in_left, in_right = halves(source[n].astype(F32), left)
            pl_l[shard * mine + n] = in_left
            pl_r[shard * mine + n] = in_right
            return carry

        lax.fori_loop(0, mine, body, 0, unroll=4)

    start(*up(0))
    start(*down(0))
    table_copies = []
    for d in range(1, rows):
        copy = pltpu.make_async_remote_copy(
            src_ref=tables.at[here], dst_ref=tables.at[here],
            send_sem=table_send.at[d - 1], recv_sem=table_recv.at[d - 1],
            device_id=(lax.rem(row + d, rows), col), device_id_type=MESH,
        )
        copy.start()
        table_copies.append(copy)
    spread(pnat_ref, row)
    turn_prolongator(left, pown_ref, order_ref, pt_l, pt_r, mine)
    for copy in table_copies:
        copy.wait()
    to_smem = pltpu.make_async_copy(tables, places, place_sem)
    to_smem.start()
    for h in range(rows - 1):
        @pl.when(row - 1 - h >= 0)
        def _():
            up(h)[1].wait_recv()

        if h + 1 < rows - 1:
            start(*up(h + 1))

        @pl.when(row + 1 + h < rows)
        def _():
            down(h)[1].wait_recv()

        if h + 1 < rows - 1:
            start(*down(h + 1))

        @pl.when(row - 1 - h >= 0)
        def _():
            spread(pg.at[row - 1 - h], row - 1 - h)

        @pl.when(row + 1 + h < rows)
        def _():
            spread(pg.at[row + 1 + h], row + 1 + h)

    to_smem.wait()

    def product_row(to, u):
        i = u * cols + to
        lhs = []
        for e in range(0, ka, 2):
            x0, x1 = a_ref[i, e].astype(F32), a_ref[i, e + 1].astype(F32)
            top = jnp.where(left, x0, swap(x1))
            bottom = jnp.where(left, swap(x0), x1)
            lhs.append(jnp.concatenate([top, bottom], axis=0).astype(BF16))
        kept = [kept_ref[i * kap + s] for s in range(kap)]
        fine = [fine_ref[i * ka + e] for e in range(ka)]
        rhs = [gather_tiles(pl_l, pl_r, [places[k, j] for j in kept]) for k in fine]
        return jnp.dot(
            jnp.concatenate(lhs, axis=1), jnp.concatenate(rhs, axis=0), preferred_element_type=F32
        )

    def coarse_row(to, n):
        j = ((n // per) * cols + to) * per + lax.rem(n, per)
        lhs = gather_tiles(pt_l, pt_r, [pidx_ref[j * own + u] for u in range(own)])
        rhs = [
            gather_tiles(apl, apr, [sidx_ref[(j * own + u) * kc + t] for t in range(kc)])
            for u in range(own)
        ]
        return jnp.dot(lhs, jnp.concatenate(rhs, axis=0), preferred_element_type=F32)

    def reduce_plane(compute, count, bufs, acc, sems):
        s1, r1, s2, r2, s1_c, r1_c, s2_c, r2_c = bufs
        s1_send, s1_recv, s2_send, s2_recv = sems
        order = list(range(1, chips)) + [0]
        first, second = [], []

        def give(n):
            d = order[n]
            to = lax.rem(chip + d, chips) * 2 + 1 - core
            slot = n % s1.shape[0]
            if n >= s1.shape[0]:
                for copy in first[n - s1.shape[0]]:
                    copy.wait_send()

            def body(k, carry):
                s1[slot, k], s1_c[slot, pl.ds(k, 1), :] = pack(compute(to, k))
                return carry

            lax.fori_loop(0, count, body, 0)
            copies = [
                pltpu.make_async_remote_copy(
                    src_ref=src.at[slot], dst_ref=dst.at[n], send_sem=s1_send.at[w, n], recv_sem=s1_recv.at[w, n],
                    device_id=(row, partner), device_id_type=MESH,
                )
                for w, (src, dst) in enumerate(((s1, r1), (s1_c, r1_c)))
            ]
            for copy in copies:
                copy.start()
            first.append(copies)

        def finish(n):
            d = order[n]
            to = lax.rem(chip + d, chips) * 2 + core
            slot = n % s2.shape[0]
            for copy in first[n]:
                copy.wait_recv()
            if d and n >= s2.shape[0]:
                for copy in second[n - s2.shape[0]]:
                    copy.wait_send()

            def body(k, carry):
                value = compute(to, k) + unpack(r1[n, k], r1_c[n, pl.ds(k, 1), :])
                if d:
                    s2[slot, k], s2_c[slot, pl.ds(k, 1), :] = pack(value)
                else:
                    acc[k] = value
                return carry

            lax.fori_loop(0, count, body, 0)
            if d:
                copies = [
                    pltpu.make_async_remote_copy(
                        src_ref=src.at[slot], dst_ref=dst.at[n], send_sem=s2_send.at[w, n], recv_sem=s2_recv.at[w, n],
                        device_id=(row, to), device_id_type=MESH,
                    )
                    for w, (src, dst) in enumerate(((s2, r2), (s2_c, r2_c)))
                ]
                for copy in copies:
                    copy.start()
                second.append(copies)

        for n in range(chips):
            give(n)
            if n:
                finish(n - 1)
        finish(chips - 1)
        for n in range(max(0, chips - s1.shape[0]), chips):
            for copy in first[n]:
                copy.wait_send()
        for copies in second:
            for copy in copies:
                copy.wait_recv()
        for n in range(max(0, chips - 1 - s2.shape[0]), chips - 1):
            for copy in second[n]:
                copy.wait_send()

        def total(k):
            value = acc[k]
            for n in range(chips - 1):
                value = value + unpack(r2[n, k], r2_c[n, pl.ds(k, 1), :])
            return value

        return total

    total = reduce_plane(
        product_row, own, (s1a, r1a, s2a, r2a, s1a_c, r1a_c, s2a_c, r2a_c), acc_a,
        (s1a_send, s1a_recv, s2a_send, s2a_recv),
    )

    def keep(u, carry):
        value = total(u).astype(BF16).astype(F32)
        for s in range(0, kap, 2):
            tile = value[:, s * width : (s + 2) * width]
            x0, x1 = interleave(tile, left)
            ap_out[u, s] = x0.astype(BF16)
            ap_out[u, s + 1] = x1.astype(BF16)
            for n, x in ((s, x0), (s + 1, x1)):
                in_left, in_right = halves(x, left)
                apl[u * kap + n] = in_left
                apr[u * kap + n] = in_right
        return carry

    lax.fori_loop(0, own, keep, 0)
    apl[own * kap] = jnp.zeros(apl.shape[1:], BF16)
    apr[own * kap] = jnp.zeros(apr.shape[1:], BF16)

    coarse_total = reduce_plane(
        coarse_row, rows * per, (s1b, r1b, s2b, r2b, s1b_c, r1b_c, s2b_c, r2b_c), acc_b,
        (s1b_send, s1b_recv, s2b_send, s2b_recv),
    )
    third = []
    for d in list(range(1, rows)) + [0]:
        to = lax.rem(row + d, rows)
        for q in range(per):
            value = coarse_total(to * per + q)
            if d:
                s3[d - 1, q], s3_c[d - 1, pl.ds(q, 1), :] = pack(value)
            else:
                mine_b[q] = value
        if d:
            for w, (src, dst) in enumerate(((s3, r3), (s3_c, r3_c))):
                copy = pltpu.make_async_remote_copy(
                    src_ref=src.at[d - 1], dst_ref=dst.at[d - 1],
                    send_sem=s3_send.at[w, d - 1], recv_sem=s3_recv.at[w, d - 1],
                    device_id=(to, col), device_id_type=MESH,
                )
                copy.start()
                third.append(copy)
    for copy in third:
        copy.wait()
    for q in range(per):
        value = mine_b[q]
        for d in range(1, rows):
            value = value + unpack(r3[d - 1, q], r3_c[d - 1, pl.ds(q, 1), :])
        for t in range(0, kc, 2):
            x0, x1 = interleave(value[:, t * width : (t + 2) * width], left)
            coarse_out[q, t] = x0
            coarse_out[q, t + 1] = x1
    for h in range(rows - 1):
        done_send(*up(h))
        done_send(*down(h))


def shards(a_blocks, a_index, p_blocks, p_index, ap_index, coarse_index):
    rows, cols = lax.axis_size("row"), lax.axis_size("col")
    count, _, ka, flat = a_blocks.shape
    own, _, kp, _ = p_blocks.shape
    kap = ap_index.shape[1]
    coarse, kc = coarse_index.shape
    per = coarse // (rows * cols)
    width = int(round(flat ** 0.5))
    half = width // 2
    lanes = 2 * width

    a2 = a_blocks.reshape(count, ka, half, lanes)
    p2 = p_blocks.reshape(own * kp, half, lanes)
    p_nat = p_blocks.reshape(own * kp, 2, half, width).transpose(0, 2, 1, 3).reshape(own * kp, half, lanes)
    groups = rows * own * kp
    across = -(-coarse // 128) * 128

    mine = p_index[:, 0]
    slots = lax.dynamic_index_in_dim(ap_index.reshape(own, cols, kap), lax.axis_index("col"), 1, keepdims=False)
    which = jnp.arange(own * kp, dtype=jnp.int32).reshape(own, kp)
    hit = mine[None] == jnp.arange(coarse, dtype=jnp.int32)[:, None, None]
    p_pick = jnp.where(jnp.any(hit, axis=2), jnp.sum(jnp.where(hit, which[None], 0), axis=2), own * kp)
    here = lax.axis_index("row") * (own * kp) + which
    sits = mine[:, :, None] == lax.broadcasted_iota(jnp.int32, (1, 1, across), 2)
    table = jnp.where(jnp.any(sits, axis=1), jnp.sum(jnp.where(sits, here[:, :, None], 0), axis=1), groups)
    spot = jnp.arange(own * kap, dtype=jnp.int32).reshape(own, kap)
    match = coarse_index[:, None, :, None] == slots[None, :, None, :]
    s_pick = jnp.where(
        jnp.any(match, axis=3), jnp.sum(jnp.where(match, spot[None, :, None, :], 0), axis=3), own * kap
    )

    into = np.arange(width)
    source = (into % half) * 2 + into // half
    order_mat = jnp.asarray(source[:, None] == np.arange(lanes)[None, :], BF16)

    chips = cols // 2
    others = max(chips - 1, 1)
    slots2 = min(others, 3)
    wide = kap * width
    wide_c = kc * width
    vmem = pl.BlockSpec(memory_space=pltpu.VMEM)
    smem = pl.BlockSpec(memory_space=pltpu.SMEM)
    dma = pltpu.SemaphoreType.DMA
    n_coarse = rows * per
    beyond = max(rows - 1, 1)

    def sums(n, across_lanes):
        depths = (2, chips, slots2, others)
        return [
            *[pltpu.VMEM((k, n, width, across_lanes), LINK) for k in depths],
            *[pltpu.VMEM((k, n, across_lanes), F32) for k in depths],
            pltpu.VMEM((n, width, across_lanes), F32),
        ]

    ap, coarse_out = pl.pallas_call(
        functools.partial(kernel, (rows, cols, own, ka, kp, kap, kc, per, groups)),
        out_shape=(
            jax.ShapeDtypeStruct((own, kap, half, lanes), BF16),
            jax.ShapeDtypeStruct((per, kc, half, lanes), F32),
        ),
        in_specs=[vmem, vmem, vmem, vmem, vmem, smem, smem, smem, smem],
        out_specs=(vmem, vmem),
        scratch_shapes=[
            pltpu.VMEM((rows, own * kp, half, lanes), BF16),
            pltpu.VMEM((rows * own, across), jnp.int32),
            pltpu.SMEM((rows * own, across), jnp.int32),
            pltpu.VMEM((groups + 1, width, lanes), BF16),
            pltpu.VMEM((groups + 1, width, lanes), BF16),
            pltpu.VMEM((own * kp + 1, width, lanes), BF16),
            pltpu.VMEM((own * kp + 1, width, lanes), BF16),
            pltpu.VMEM((own * kap + 1, width, lanes), BF16),
            pltpu.VMEM((own * kap + 1, width, lanes), BF16),
            *sums(own, wide),
            *sums(n_coarse, wide_c),
            pltpu.VMEM((per, width, wide_c), F32),
            pltpu.VMEM((beyond, per, width, wide_c), LINK),
            pltpu.VMEM((beyond, per, width, wide_c), LINK),
            pltpu.VMEM((beyond, per, wide_c), F32),
            pltpu.VMEM((beyond, per, wide_c), F32),
            dma((beyond,)), dma((beyond,)), dma((beyond,)), dma((beyond,)), dma((beyond,)), dma((beyond,)), dma,
            dma((2, chips)), dma((2, chips)), dma((2, others)), dma((2, others)),
            dma((2, chips)), dma((2, chips)), dma((2, others)), dma((2, others)),
            dma((2, beyond)), dma((2, beyond)),
        ],
        compiler_params=pltpu.CompilerParams(
            collective_id=0, has_side_effects=True, vmem_limit_bytes=60 * 1024 * 1024
        ),
    )(a2, p_nat, p2, order_mat, table, a_index.reshape(-1), ap_index.reshape(-1), p_pick.reshape(-1), s_pick.reshape(-1))
    return ap.reshape(own, 1, kap, flat), coarse_out.reshape(per, kc, flat)


def solution(mesh):
    placed = (
        P("row", "col", None, None),
        P("row", "col", None),
        P("row", "col", None, None),
        P("row", "col", None),
        P("row", None),
        P(),
    )
    return jax.shard_map(
        shards,
        mesh=mesh,
        in_specs=placed,
        out_specs=(P("row", "col", None, None), P(("row", "col"), None, None)),
        check_vma=False,
    )
```

```python
import functools

import jax
import jax.numpy as jnp
from jax import lax
from jax.experimental import pallas as pl
from jax.experimental.pallas import tpu as pltpu
from jax.sharding import PartitionSpec as P

MESH = pl.DeviceIdType.MESH
F32 = jnp.float32
BF16 = jnp.bfloat16
LINK = jnp.int16
TOP = 32766.0


def left_mask(half):
    return lax.broadcasted_iota(jnp.int32, (half, 4 * half), 1) < 2 * half


def swap(x):
    return pltpu.roll(x, x.shape[1] // 2, 1)


def halves(x, left):
    other = swap(x)
    zero = jnp.zeros_like(x)
    in_left = jnp.concatenate([jnp.where(left, x, zero), jnp.where(left, other, zero)], axis=0)
    in_right = jnp.concatenate([jnp.where(left, zero, other), jnp.where(left, zero, x)], axis=0)
    return in_left.astype(BF16), in_right.astype(BF16)


def interleave(tile, left):
    half = left.shape[0]
    top, bottom = tile[:half], tile[half:]
    return jnp.where(left, top, swap(bottom)), jnp.where(left, swap(top), bottom)


def pack(value):
    most = jnp.maximum(jnp.max(jnp.abs(value), axis=0, keepdims=True), 1e-30)
    return jnp.round(value * (TOP / most)).astype(jnp.int32).astype(LINK), most * (1.0 / TOP)


def unpack(value, scale):
    return value.astype(jnp.int32).astype(F32) * scale


def gather_tiles(in_left, in_right, picks):
    return jnp.concatenate(
        [in_left[picks[n]] + in_right[picks[n + 1]] for n in range(0, len(picks), 2)], axis=1
    )


def turn_prolongator(left, own_ref, pt_l, pt_r, mine):
    half, lanes = left.shape
    into = lax.broadcasted_iota(jnp.int32, (2 * half, lanes), 0)
    source = lax.rem(into, half) * 2 + into // half
    order_mat = (source == lax.broadcasted_iota(jnp.int32, (2 * half, lanes), 1)).astype(F32).astype(BF16)
    contract = (((1,), (1,)), ((), ()))

    def body(n, carry):
        block = halves(own_ref[n].astype(F32), left)[0]
        zero = jnp.zeros_like(block)
        for ref, pair in ((pt_l, [block, zero]), (pt_r, [zero, block])):
            ref[n] = lax.dot_general(
                order_mat, jnp.concatenate(pair, axis=0), contract, preferred_element_type=F32
            ).astype(BF16)
        return carry

    lax.fori_loop(0, mine, body, 0, unroll=4)
    pt_l[mine] = jnp.zeros(pt_l.shape[1:], BF16)
    pt_r[mine] = jnp.zeros(pt_r.shape[1:], BF16)


def to_rows(flat, out, half):
    n, lanes = flat.shape[0], out.shape[1]
    for j in range(half):
        out[pl.ds(j, n, stride=half), :] = flat[:, j * lanes : (j + 1) * lanes]


def to_flat(rows_ref, n, half, j):
    return rows_ref[pl.ds(j, n, stride=half), :]


def kernel(
    sizes, a_ref, p_ref, fine_ref, pcol_ref, kept_ref, cols_ref,
    ap_out, coarse_out,
    a_pre, pg, tables, local, spots, places, local_places, spot_places, rows_in, rows_out,
    pl_l, pl_r, pt_l, pt_r, apl, apr,
    s1a, r1a, s2a, r2a, s1a_c, r1a_c, s2a_c, r2a_c, acc_a,
    s1b, r1b, s2b, r2b, s1b_c, r1b_c, s2b_c, r2b_c, acc_b, mine_b, s3, r3, s3_c, r3_c,
    up_send, up_recv, down_send, down_recv, table_send, table_recv, place_sem,
    s1a_send, s1a_recv, s2a_send, s2a_recv, s1b_send, s1b_recv, s2b_send, s2b_recv, s3_send, s3_recv,
):
    rows, cols, own, ka, kp, kap, kc, per, groups = sizes
    chips = cols // 2
    half = pg.shape[2]
    width = 2 * half
    left = left_mask(half)
    row, col = lax.axis_index("row"), lax.axis_index("col")
    core = lax.rem(col, 2)
    chip = col // 2
    partner = chip * 2 + 1 - core

    barrier = pltpu.get_barrier_semaphore()
    pl.semaphore_signal(barrier, inc=1, device_id=(row, partner), device_id_type=MESH)
    for d in range(1, chips):
        there = lax.rem(chip + d, chips) * 2 + core
        pl.semaphore_signal(barrier, inc=1, device_id=(row, there), device_id_type=MESH)
    for d in range(1, rows):
        pl.semaphore_signal(
            barrier, inc=1, device_id=(lax.rem(row + d, rows), col), device_id_type=MESH
        )

    mine = own * kp

    def lay_out(u, carry):
        to_rows(p_ref[u, 0].astype(F32), rows_in.at[0], half)
        for m in range(kp):
            pg[row, u * kp + m] = rows_in[0, m * half : (m + 1) * half, :].astype(BF16)
        return carry

    lax.fori_loop(0, own, lay_out, 0)
    lane = lax.broadcasted_iota(jnp.int32, (1, tables.shape[1]), 1)
    lines = []
    for u in range(own):
        line = jnp.full(lane.shape, mine, jnp.int32)
        for m in range(kp):
            line = jnp.where(lane == pcol_ref[u, 0, m], u * kp + m, line)
        lines.append(line)
        spot = jnp.full(lane.shape, own * kap, jnp.int32)
        for n in range(kap):
            spot = jnp.where(lane == kept_ref[u * cols + col, n], u * kap + n, spot)
        spots[u : u + 1, :] = spot
    lines = jnp.concatenate(lines, axis=0)
    local[...] = lines
    here = pl.ds(pl.multiple_of(row * own, own), own)
    tables[here, :] = jnp.where(lines < mine, lines + row * mine, groups)
    pl_l[groups] = jnp.zeros(pl_l.shape[1:], BF16)
    pl_r[groups] = jnp.zeros(pl_r.shape[1:], BF16)
    pl.semaphore_wait(barrier, chips + rows - 1)

    def up(h):
        shard = row - h
        return (shard >= 0) & (row + 1 < rows), pltpu.make_async_remote_copy(
            src_ref=pg.at[shard], dst_ref=pg.at[shard],
            send_sem=up_send.at[h], recv_sem=up_recv.at[h],
            device_id=(row + 1, col), device_id_type=MESH,
        )

    def down(h):
        shard = row + h
        return (shard < rows) & (row > 0), pltpu.make_async_remote_copy(
            src_ref=pg.at[shard], dst_ref=pg.at[shard],
            send_sem=down_send.at[h], recv_sem=down_recv.at[h],
            device_id=(row - 1, col), device_id_type=MESH,
        )

    def start(ready, copy):
        @pl.when(ready)
        def _():
            copy.start()

    def done_send(ready, copy):
        @pl.when(ready)
        def _():
            copy.wait_send()

    into = lax.broadcasted_iota(jnp.int32, (width, width), 0)
    natural = lax.rem(into, 2) * half + into // 2 == lax.broadcasted_iota(jnp.int32, (width, width), 1)
    natural = natural.astype(F32).astype(BF16)

    def spread(shard):
        def body(n, carry):
            pair = jnp.concatenate(halves(pg[shard, n].astype(F32), left), axis=1)
            pair = jnp.dot(natural, pair, preferred_element_type=F32).astype(BF16)
            pl_l[shard * mine + n] = pair[:, : 2 * width]
            pl_r[shard * mine + n] = pair[:, 2 * width :]
            return carry

        lax.fori_loop(0, mine, body, 0, unroll=4)

    start(*up(0))
    start(*down(0))
    table_copies = []
    for d in range(1, rows):
        copy = pltpu.make_async_remote_copy(
            src_ref=tables.at[here], dst_ref=tables.at[here],
            send_sem=table_send.at[d - 1], recv_sem=table_recv.at[d - 1],
            device_id=(lax.rem(row + d, rows), col), device_id_type=MESH,
        )
        copy.start()
        table_copies.append(copy)
    small = [
        pltpu.make_async_copy(local, local_places, place_sem.at[0]),
        pltpu.make_async_copy(spots, spot_places, place_sem.at[1]),
    ]
    for copy in small:
        copy.start()

    def lay_rows(n, carry):
        for k in range(2):
            i = n * 2 + k
            to_rows(a_ref[i, 0].astype(F32), rows_in.at[k], half)
            for e in range(0, ka, 2):
                x0 = rows_in[k, e * half : (e + 1) * half, :]
                x1 = rows_in[k, (e + 1) * half : (e + 2) * half, :]
                top = jnp.where(left, x0, swap(x1))
                bottom = jnp.where(left, swap(x0), x1)
                tile = jnp.concatenate([top, bottom], axis=0).astype(BF16)
                a_pre[i, :, e * width : (e + 2) * width] = tile
        return carry

    lax.fori_loop(0, a_ref.shape[0] // 2, lay_rows, 0)
    spread(row)
    turn_prolongator(left, pg.at[row], pt_l, pt_r, mine)
    for copy in table_copies:
        copy.wait()
    small.append(pltpu.make_async_copy(tables, places, place_sem.at[2]))
    small[2].start()
    for h in range(rows - 1):
        @pl.when(row - 1 - h >= 0)
        def _():
            up(h)[1].wait_recv()

        if h + 1 < rows - 1:
            start(*up(h + 1))

        @pl.when(row + 1 + h < rows)
        def _():
            down(h)[1].wait_recv()

        if h + 1 < rows - 1:
            start(*down(h + 1))

        @pl.when(row - 1 - h >= 0)
        def _():
            spread(row - 1 - h)

        @pl.when(row + 1 + h < rows)
        def _():
            spread(row + 1 + h)

    for copy in small:
        copy.wait()

    def product_row(to, u):
        i = u * cols + to
        kept = [kept_ref[i, n] for n in range(kap)]
        fine = [fine_ref[i, 0, e] for e in range(ka)]
        rhs = [gather_tiles(pl_l, pl_r, [places[k, j] for j in kept]) for k in fine]
        return jnp.dot(a_pre[i], jnp.concatenate(rhs, axis=0), preferred_element_type=F32)

    def coarse_row(to, n):
        j = ((n // per) * cols + to) * per + lax.rem(n, per)
        lhs = gather_tiles(pt_l, pt_r, [local_places[u, j] for u in range(own)])
        kept = [cols_ref[j, t] for t in range(kc)]
        rhs = [gather_tiles(apl, apr, [spot_places[u, c] for c in kept]) for u in range(own)]
        return jnp.dot(lhs, jnp.concatenate(rhs, axis=0), preferred_element_type=F32)

    def reduce_plane(compute, count, bufs, acc, sems):
        s1, r1, s2, r2, s1_c, r1_c, s2_c, r2_c = bufs
        s1_send, s1_recv, s2_send, s2_recv = sems
        order = list(range(1, chips)) + [0]
        first, second = [], []

        def give(n):
            d = order[n]
            to = lax.rem(chip + d, chips) * 2 + 1 - core
            slot = n % s1.shape[0]
            if n >= s1.shape[0]:
                for copy in first[n - s1.shape[0]]:
                    copy.wait_send()

            def body(k, carry):
                s1[slot, k], s1_c[slot, pl.ds(k, 1), :] = pack(compute(to, k))
                return carry

            lax.fori_loop(0, count, body, 0, unroll=2)
            copies = [
                pltpu.make_async_remote_copy(
                    src_ref=src.at[slot], dst_ref=dst.at[n], send_sem=s1_send.at[w, n], recv_sem=s1_recv.at[w, n],
                    device_id=(row, partner), device_id_type=MESH,
                )
                for w, (src, dst) in enumerate(((s1, r1), (s1_c, r1_c)))
            ]
            for copy in copies:
                copy.start()
            first.append(copies)

        def finish(n):
            d = order[n]
            to = lax.rem(chip + d, chips) * 2 + core
            slot = n % s2.shape[0]
            for copy in first[n]:
                copy.wait_recv()
            if d and n >= s2.shape[0]:
                for copy in second[n - s2.shape[0]]:
                    copy.wait_send()

            def body(k, carry):
                value = compute(to, k) + unpack(r1[n, k], r1_c[n, pl.ds(k, 1), :])
                if d:
                    s2[slot, k], s2_c[slot, pl.ds(k, 1), :] = pack(value)
                else:
                    acc[k] = value
                return carry

            lax.fori_loop(0, count, body, 0, unroll=2)
            if d:
                copies = [
                    pltpu.make_async_remote_copy(
                        src_ref=src.at[slot], dst_ref=dst.at[n], send_sem=s2_send.at[w, n], recv_sem=s2_recv.at[w, n],
                        device_id=(row, to), device_id_type=MESH,
                    )
                    for w, (src, dst) in enumerate(((s2, r2), (s2_c, r2_c)))
                ]
                for copy in copies:
                    copy.start()
                second.append(copies)

        for n in range(chips):
            give(n)
            if n:
                finish(n - 1)
        finish(chips - 1)
        for n in range(max(0, chips - s1.shape[0]), chips):
            for copy in first[n]:
                copy.wait_send()
        for copies in second:
            for copy in copies:
                copy.wait_recv()
        for n in range(max(0, chips - 1 - s2.shape[0]), chips - 1):
            for copy in second[n]:
                copy.wait_send()

        def total(k):
            value = acc[k]
            for n in range(chips - 1):
                value = value + unpack(r2[n, k], r2_c[n, pl.ds(k, 1), :])
            return value

        return total

    total = reduce_plane(
        product_row, own, (s1a, r1a, s2a, r2a, s1a_c, r1a_c, s2a_c, r2a_c), acc_a,
        (s1a_send, s1a_recv, s2a_send, s2a_recv),
    )

    def keep(u, carry):
        value = total(u).astype(BF16).astype(F32)
        for s in range(0, kap, 2):
            tile = value[:, s * width : (s + 2) * width]
            x0, x1 = interleave(tile, left)
            rows_out[s * half : (s + 1) * half, :] = x0
            rows_out[(s + 1) * half : (s + 2) * half, :] = x1
            for n, x in ((s, x0), (s + 1, x1)):
                in_left, in_right = halves(x, left)
                apl[u * kap + n] = in_left
                apr[u * kap + n] = in_right
        for j in range(half):
            ap_out[u, 0, :, j * 2 * width : (j + 1) * 2 * width] = to_flat(rows_out, kap, half, j).astype(BF16)
        return carry

    lax.fori_loop(0, own, keep, 0)
    apl[own * kap] = jnp.zeros(apl.shape[1:], BF16)
    apr[own * kap] = jnp.zeros(apr.shape[1:], BF16)

    coarse_total = reduce_plane(
        coarse_row, rows * per, (s1b, r1b, s2b, r2b, s1b_c, r1b_c, s2b_c, r2b_c), acc_b,
        (s1b_send, s1b_recv, s2b_send, s2b_recv),
    )
    third = []
    for d in list(range(1, rows)) + [0]:
        to = lax.rem(row + d, rows)
        for q in range(per):
            value = coarse_total(to * per + q)
            if d:
                s3[d - 1, q], s3_c[d - 1, pl.ds(q, 1), :] = pack(value)
            else:
                mine_b[q] = value
        if d:
            for w, (src, dst) in enumerate(((s3, r3), (s3_c, r3_c))):
                copy = pltpu.make_async_remote_copy(
                    src_ref=src.at[d - 1], dst_ref=dst.at[d - 1],
                    send_sem=s3_send.at[w, d - 1], recv_sem=s3_recv.at[w, d - 1],
                    device_id=(to, col), device_id_type=MESH,
                )
                copy.start()
                third.append(copy)
    for copy in third:
        copy.wait()
    for q in range(per):
        value = mine_b[q]
        for d in range(1, rows):
            value = value + unpack(r3[d - 1, q], r3_c[d - 1, pl.ds(q, 1), :])
        for t in range(0, kc, 2):
            x0, x1 = interleave(value[:, t * width : (t + 2) * width], left)
            rows_out[t * half : (t + 1) * half, :] = x0
            rows_out[(t + 1) * half : (t + 2) * half, :] = x1
        for j in range(half):
            coarse_out[q, :, j * 2 * width : (j + 1) * 2 * width] = to_flat(rows_out, kc, half, j)
    for h in range(rows - 1):
        done_send(*up(h))
        done_send(*down(h))


def shards(a_blocks, a_index, p_blocks, p_index, ap_index, coarse_index):
    rows, cols = lax.axis_size("row"), lax.axis_size("col")
    count, _, ka, flat = a_blocks.shape
    own, _, kp, _ = p_blocks.shape
    kap = ap_index.shape[1]
    coarse, kc = coarse_index.shape
    per = coarse // (rows * cols)
    width = int(round(flat ** 0.5))
    half = width // 2
    lanes = 2 * width

    groups = rows * own * kp
    across = -(-coarse // 128) * 128
    chips = cols // 2
    others = max(chips - 1, 1)
    slots2 = min(others, 3)
    wide = kap * width
    wide_c = kc * width
    vmem = pl.BlockSpec(memory_space=pltpu.VMEM)
    smem = pl.BlockSpec(memory_space=pltpu.SMEM)
    dma = pltpu.SemaphoreType.DMA
    n_coarse = rows * per
    beyond = max(rows - 1, 1)

    def sums(n, across_lanes):
        depths = (2, chips, slots2, others)
        return [
            *[pltpu.VMEM((k, n, width, across_lanes), LINK) for k in depths],
            *[pltpu.VMEM((k, n, across_lanes), F32) for k in depths],
            pltpu.VMEM((n, width, across_lanes), F32),
        ]

    ap, coarse_out = pl.pallas_call(
        functools.partial(kernel, (rows, cols, own, ka, kp, kap, kc, per, groups)),
        out_shape=(
            jax.ShapeDtypeStruct((own, 1, kap, flat), BF16),
            jax.ShapeDtypeStruct((per, kc, flat), F32),
        ),
        in_specs=[vmem, vmem, smem, smem, smem, smem],
        out_specs=(vmem, vmem),
        scratch_shapes=[
            pltpu.VMEM((count, width, ka * width), BF16),
            pltpu.VMEM((rows, own * kp, half, lanes), BF16),
            pltpu.VMEM((rows * own, across), jnp.int32),
            pltpu.VMEM((own, across), jnp.int32),
            pltpu.VMEM((own, across), jnp.int32),
            pltpu.SMEM((rows * own, across), jnp.int32),
            pltpu.SMEM((own, across), jnp.int32),
            pltpu.SMEM((own, across), jnp.int32),
            pltpu.VMEM((2, max(ka, kp) * half, lanes), F32),
            pltpu.VMEM((max(kap, kc) * half, lanes), F32),
            pltpu.VMEM((groups + 1, width, lanes), BF16),
            pltpu.VMEM((groups + 1, width, lanes), BF16),
            pltpu.VMEM((own * kp + 1, width, lanes), BF16),
            pltpu.VMEM((own * kp + 1, width, lanes), BF16),
            pltpu.VMEM((own * kap + 1, width, lanes), BF16),
            pltpu.VMEM((own * kap + 1, width, lanes), BF16),
            *sums(own, wide),
            *sums(n_coarse, wide_c),
            pltpu.VMEM((per, width, wide_c), F32),
            pltpu.VMEM((beyond, per, width, wide_c), LINK),
            pltpu.VMEM((beyond, per, width, wide_c), LINK),
            pltpu.VMEM((beyond, per, wide_c), F32),
            pltpu.VMEM((beyond, per, wide_c), F32),
            dma((beyond,)), dma((beyond,)), dma((beyond,)), dma((beyond,)), dma((beyond,)), dma((beyond,)), dma((3,)),
            dma((2, chips)), dma((2, chips)), dma((2, others)), dma((2, others)),
            dma((2, chips)), dma((2, chips)), dma((2, others)), dma((2, others)),
            dma((2, beyond)), dma((2, beyond)),
        ],
        compiler_params=pltpu.CompilerParams(
            collective_id=0, has_side_effects=True, vmem_limit_bytes=60 * 1024 * 1024
        ),
    )(a_blocks, p_blocks, a_index, p_index, ap_index, coarse_index)
    return ap, coarse_out


def solution(mesh):
    placed = (
        P("row", "col", None, None),
        P("row", "col", None),
        P("row", "col", None, None),
        P("row", "col", None),
        P("row", None),
        P(),
    )
    return jax.shard_map(
        shards,
        mesh=mesh,
        in_specs=placed,
        out_specs=(P("row", "col", None, None), P(("row", "col"), None, None)),
        check_vma=False,
    )
```

```python
import functools

import jax
import jax.numpy as jnp
from jax import lax
from jax.experimental import pallas as pl
from jax.experimental.pallas import tpu as pltpu
from jax.sharding import PartitionSpec as P

MESH = pl.DeviceIdType.MESH
F32 = jnp.float32
BF16 = jnp.bfloat16
LINK = jnp.int16
TOP = 32766.0


def left_mask(half):
    return lax.broadcasted_iota(jnp.int32, (half, 4 * half), 1) < 2 * half


def swap(x):
    return pltpu.roll(x, x.shape[1] // 2, 1)


def halves(x, left):
    other = swap(x)
    zero = jnp.zeros_like(x)
    in_left = jnp.concatenate([jnp.where(left, x, zero), jnp.where(left, other, zero)], axis=0)
    in_right = jnp.concatenate([jnp.where(left, zero, other), jnp.where(left, zero, x)], axis=0)
    return in_left.astype(BF16), in_right.astype(BF16)


def interleave(tile, left):
    half = left.shape[0]
    top, bottom = tile[:half], tile[half:]
    return jnp.where(left, top, swap(bottom)), jnp.where(left, swap(top), bottom)


def pack(value):
    most = jnp.maximum(jnp.max(jnp.abs(value), axis=0, keepdims=True), 1e-30)
    return jnp.round(value * (TOP / most)).astype(jnp.int32).astype(LINK), most * (1.0 / TOP)


def unpack(value, scale):
    return value.astype(jnp.int32).astype(F32) * scale


def pieces_of(count):
    return 2 if count % 2 == 0 else 1


def gather_tiles(in_left, in_right, picks):
    return jnp.concatenate(
        [in_left[picks[n]] + in_right[picks[n + 1]] for n in range(0, len(picks), 2)], axis=1
    )


def turn_prolongator(left, own_ref, pt_l, pt_r, mine):
    half, lanes = left.shape
    into = lax.broadcasted_iota(jnp.int32, (2 * half, lanes), 0)
    source = lax.rem(into, half) * 2 + into // half
    order_mat = (source == lax.broadcasted_iota(jnp.int32, (2 * half, lanes), 1)).astype(F32).astype(BF16)
    contract = (((1,), (1,)), ((), ()))

    def body(n, carry):
        block = halves(own_ref[n].astype(F32), left)[0]
        zero = jnp.zeros_like(block)
        for ref, pair in ((pt_l, [block, zero]), (pt_r, [zero, block])):
            ref[n] = lax.dot_general(
                order_mat, jnp.concatenate(pair, axis=0), contract, preferred_element_type=F32
            ).astype(BF16)
        return carry

    lax.fori_loop(0, mine, body, 0, unroll=4)
    pt_l[mine] = jnp.zeros(pt_l.shape[1:], BF16)
    pt_r[mine] = jnp.zeros(pt_r.shape[1:], BF16)


def to_rows(flat, out, half):
    n, lanes = flat.shape[0], out.shape[1]
    for j in range(half):
        out[pl.ds(j, n, stride=half), :] = flat[:, j * lanes : (j + 1) * lanes]


def to_flat(rows_ref, n, half, j):
    return rows_ref[pl.ds(j, n, stride=half), :]


def kernel(
    sizes, a_ref, p_ref, fine_any, pcol_any, kept_any, cols_any,
    ap_out, coarse_out,
    fine_ref, pcol_ref, kept_ref, cols_ref, a_pre, pg, tables, local, spots, places, local_places, spot_places, rows_in, rows_out,
    pl_l, pl_r, pt_l, pt_r, apl, apr,
    s1a, r1a, s2a, r2a, s1a_c, r1a_c, s2a_c, r2a_c, acc_a,
    s1b, r1b, s2b, r2b, s1b_c, r1b_c, s2b_c, r2b_c, acc_b, mine_b, s3, r3, s3_c, r3_c,
    up_send, up_recv, down_send, down_recv, table_send, table_recv, place_sem,
    s1a_send, s1a_recv, s2a_send, s2a_recv, s1b_send, s1b_recv, s2b_send, s2b_recv, s3_send, s3_recv,
):
    rows, cols, own, ka, kp, kap, kc, per, groups = sizes
    chips = cols // 2
    half = pg.shape[2]
    width = 2 * half
    left = left_mask(half)
    row, col = lax.axis_index("row"), lax.axis_index("col")
    core = lax.rem(col, 2)
    chip = col // 2
    partner = chip * 2 + 1 - core

    barrier = pltpu.get_barrier_semaphore()
    pl.semaphore_signal(barrier, inc=1, device_id=(row, partner), device_id_type=MESH)
    for d in range(1, chips):
        there = lax.rem(chip + d, chips) * 2 + core
        pl.semaphore_signal(barrier, inc=1, device_id=(row, there), device_id_type=MESH)
    for d in range(1, rows):
        pl.semaphore_signal(
            barrier, inc=1, device_id=(lax.rem(row + d, rows), col), device_id_type=MESH
        )

    mine = own * kp
    indices = [
        pltpu.make_async_copy(src, dst, place_sem.at[3 + n])
        for n, (src, dst) in enumerate(
            ((fine_any, fine_ref), (pcol_any, pcol_ref), (kept_any, kept_ref), (cols_any, cols_ref))
        )
    ]
    for copy in indices:
        copy.start()

    def lay_out(u, carry):
        to_rows(p_ref[u, 0].astype(F32), rows_in.at[0], half)
        for m in range(kp):
            pg[row, u * kp + m] = rows_in[0, m * half : (m + 1) * half, :].astype(BF16)
        return carry

    lax.fori_loop(0, own, lay_out, 0)
    pl.semaphore_wait(barrier, chips + rows - 1)

    def up(h):
        shard = row - h
        return (shard >= 0) & (row + 1 < rows), pltpu.make_async_remote_copy(
            src_ref=pg.at[shard], dst_ref=pg.at[shard],
            send_sem=up_send.at[h], recv_sem=up_recv.at[h],
            device_id=(row + 1, col), device_id_type=MESH,
        )

    def down(h):
        shard = row + h
        return (shard < rows) & (row > 0), pltpu.make_async_remote_copy(
            src_ref=pg.at[shard], dst_ref=pg.at[shard],
            send_sem=down_send.at[h], recv_sem=down_recv.at[h],
            device_id=(row - 1, col), device_id_type=MESH,
        )

    def start(ready, copy):
        @pl.when(ready)
        def _():
            copy.start()

    def done_send(ready, copy):
        @pl.when(ready)
        def _():
            copy.wait_send()

    into = lax.broadcasted_iota(jnp.int32, (width, width), 0)
    natural = lax.rem(into, 2) * half + into // 2 == lax.broadcasted_iota(jnp.int32, (width, width), 1)
    natural = natural.astype(F32).astype(BF16)

    def spread(shard):
        def body(n, carry):
            pair = jnp.concatenate(halves(pg[shard, n].astype(F32), left), axis=1)
            pair = jnp.dot(natural, pair, preferred_element_type=F32).astype(BF16)
            pl_l[shard * mine + n] = pair[:, : 2 * width]
            pl_r[shard * mine + n] = pair[:, 2 * width :]
            return carry

        lax.fori_loop(0, mine, body, 0, unroll=4)

    start(*up(0))
    start(*down(0))
    for copy in indices:
        copy.wait()
    lane = lax.broadcasted_iota(jnp.int32, (1, tables.shape[1]), 1)
    lines = []
    for u in range(own):
        line = jnp.full(lane.shape, mine, jnp.int32)
        for m in range(kp):
            line = jnp.where(lane == pcol_ref[u, 0, m], u * kp + m, line)
        lines.append(line)
        spot = jnp.full(lane.shape, own * kap, jnp.int32)
        for n in range(kap):
            spot = jnp.where(lane == kept_ref[u * cols + col, n], u * kap + n, spot)
        spots[u : u + 1, :] = spot
    lines = jnp.concatenate(lines, axis=0)
    local[...] = lines
    here = pl.ds(pl.multiple_of(row * own, own), own)
    tables[here, :] = jnp.where(lines < mine, lines + row * mine, groups)
    pl_l[groups] = jnp.zeros(pl_l.shape[1:], BF16)
    pl_r[groups] = jnp.zeros(pl_r.shape[1:], BF16)
    table_copies = []
    for d in range(1, rows):
        copy = pltpu.make_async_remote_copy(
            src_ref=tables.at[here], dst_ref=tables.at[here],
            send_sem=table_send.at[d - 1], recv_sem=table_recv.at[d - 1],
            device_id=(lax.rem(row + d, rows), col), device_id_type=MESH,
        )
        copy.start()
        table_copies.append(copy)
    small = [
        pltpu.make_async_copy(local, local_places, place_sem.at[0]),
        pltpu.make_async_copy(spots, spot_places, place_sem.at[1]),
    ]
    for copy in small:
        copy.start()

    def lay_rows(n, carry):
        for k in range(2):
            i = n * 2 + k
            to_rows(a_ref[i, 0].astype(F32), rows_in.at[k], half)
            for e in range(0, ka, 2):
                x0 = rows_in[k, e * half : (e + 1) * half, :]
                x1 = rows_in[k, (e + 1) * half : (e + 2) * half, :]
                top = jnp.where(left, x0, swap(x1))
                bottom = jnp.where(left, swap(x0), x1)
                tile = jnp.concatenate([top, bottom], axis=0).astype(BF16)
                a_pre[i, :, e * width : (e + 2) * width] = tile
        return carry

    lax.fori_loop(0, a_ref.shape[0] // 2, lay_rows, 0)
    spread(row)
    turn_prolongator(left, pg.at[row], pt_l, pt_r, mine)
    for copy in table_copies:
        copy.wait()
    small.append(pltpu.make_async_copy(tables, places, place_sem.at[2]))
    small[2].start()
    for h in range(rows - 1):
        @pl.when(row - 1 - h >= 0)
        def _():
            up(h)[1].wait_recv()

        if h + 1 < rows - 1:
            start(*up(h + 1))

        @pl.when(row + 1 + h < rows)
        def _():
            down(h)[1].wait_recv()

        if h + 1 < rows - 1:
            start(*down(h + 1))

        @pl.when(row - 1 - h >= 0)
        def _():
            spread(row - 1 - h)

        @pl.when(row + 1 + h < rows)
        def _():
            spread(row + 1 + h)

    for copy in small:
        copy.wait()

    def product_row(to, u):
        i = u * cols + to
        kept = [kept_ref[i, n] for n in range(kap)]
        fine = [fine_ref[i, 0, e] for e in range(ka)]
        rhs = [gather_tiles(pl_l, pl_r, [places[k, j] for j in kept]) for k in fine]
        return jnp.dot(a_pre[i], jnp.concatenate(rhs, axis=0), preferred_element_type=F32)

    def coarse_row(to, n):
        j = ((n // per) * cols + to) * per + lax.rem(n, per)
        lhs = gather_tiles(pt_l, pt_r, [local_places[u, j] for u in range(own)])
        kept = [cols_ref[j, t] for t in range(kc)]
        rhs = [gather_tiles(apl, apr, [spot_places[u, c] for c in kept]) for u in range(own)]
        return jnp.dot(lhs, jnp.concatenate(rhs, axis=0), preferred_element_type=F32)

    nx = 2 if chips % 2 == 0 else 1
    ny = chips // nx
    chip_y, chip_x = chip // nx, lax.rem(chip, nx)

    def column(step, on):
        return (lax.rem(chip_y + step[0], ny) * nx + lax.rem(chip_x + step[1], nx)) * 2 + on

    def reduce_plane(compute, count, bufs, acc, sems):
        s1, r1, s2, r2, s1_c, r1_c, s2_c, r2_c = bufs
        s1_send, s1_recv, s2_send, s2_recv = sems
        pieces = pieces_of(count)
        size = count // pieces
        far = [(dy, 1) for dy in range(1, ny)] if nx == 2 else []
        along_x = [(0, 1)] if nx == 2 else []
        along_y = [(dy, 0) for dy in range(1, ny)]
        plan = []
        for leg in range(4):
            for p in range(pieces):
                x_first = p % 2 == 0
                if leg == 0:
                    plan += [(p, d, (0, 1) if x_first else (d[0], 0), []) for d in far]
                elif leg == 1:
                    plan += [(p, d, d, []) for d in (along_x if x_first else along_y)]
                elif leg == 2 and x_first:
                    plan += [(p, d, d, [(d[0], 1)] if far else []) for d in along_y]
                elif leg == 2:
                    plan += [(p, d, d, far) for d in along_x]
                else:
                    plan.append((p, (0, 0), None, along_x + along_y))
        first, second, place = [], [], {}

        def start(src, dst, slot, n, send, recv, device):
            copies = [
                pltpu.make_async_remote_copy(
                    src_ref=a.at[slot], dst_ref=b.at[n], send_sem=send.at[w, n], recv_sem=recv.at[w, n],
                    device_id=(row, device), device_id_type=MESH,
                )
                for w, (a, b) in enumerate(zip(src, dst))
            ]
            for copy in copies:
                copy.start()
            return copies

        def give(n):
            p, d = plan[n][:2]
            to = column(d, 1 - core)
            slot = n % s1.shape[0]
            if n >= s1.shape[0]:
                for copy in first[n - s1.shape[0]]:
                    copy.wait_send()

            def body(k, carry):
                s1[slot, k], s1_c[slot, pl.ds(k, 1), :] = pack(compute(to, p * size + k))
                return carry

            lax.fori_loop(0, size, body, 0, unroll=2)
            first.append(start((s1, s1_c), (r1, r1_c), slot, n, s1_send, s1_recv, partner))

        def arrived(p, adds):
            slots = [place[p, d] for d in adds]
            for m in slots:
                for copy in second[m]:
                    copy.wait_recv()
            return slots

        def finish(n):
            p, d, via, adds = plan[n]
            to = column(d, core)
            m = len(second)
            slot = m % s2.shape[0]
            for copy in first[n]:
                copy.wait_recv()
            slots = arrived(p, adds) if via else []
            if via and m >= s2.shape[0]:
                for copy in second[m - s2.shape[0]]:
                    copy.wait_send()

            def body(k, carry):
                value = compute(to, p * size + k) + unpack(r1[n, k], r1_c[n, pl.ds(k, 1), :])
                for other in slots:
                    value = value + unpack(r2[other, k], r2_c[other, pl.ds(k, 1), :])
                if via:
                    s2[slot, k], s2_c[slot, pl.ds(k, 1), :] = pack(value)
                else:
                    acc[p * size + k] = value
                return carry

            lax.fori_loop(0, size, body, 0, unroll=2)
            if via:
                place[p, d] = m
                second.append(start((s2, s2_c), (r2, r2_c), slot, m, s2_send, s2_recv, column(via, core)))

        for n in range(len(plan)):
            give(n)
            if n:
                finish(n - 1)
        finish(len(plan) - 1)
        for p, _, via, adds in plan:
            if via is None:
                slots = arrived(p, adds)

                def body(k, carry):
                    value = acc[p * size + k]
                    for other in slots:
                        value = value + unpack(r2[other, k], r2_c[other, pl.ds(k, 1), :])
                    acc[p * size + k] = value
                    return carry

                lax.fori_loop(0, size, body, 0, unroll=2)
        for copies in first[-s1.shape[0]:] + second[-s2.shape[0]:]:
            for copy in copies:
                copy.wait_send()

    reduce_plane(
        product_row, own, (s1a, r1a, s2a, r2a, s1a_c, r1a_c, s2a_c, r2a_c), acc_a,
        (s1a_send, s1a_recv, s2a_send, s2a_recv),
    )

    def keep(u, carry):
        value = acc_a[u].astype(BF16).astype(F32)
        for s in range(0, kap, 2):
            tile = value[:, s * width : (s + 2) * width]
            x0, x1 = interleave(tile, left)
            rows_out[s * half : (s + 1) * half, :] = x0
            rows_out[(s + 1) * half : (s + 2) * half, :] = x1
            for n, x in ((s, x0), (s + 1, x1)):
                in_left, in_right = halves(x, left)
                apl[u * kap + n] = in_left
                apr[u * kap + n] = in_right
        for j in range(half):
            ap_out[u, 0, :, j * 2 * width : (j + 1) * 2 * width] = to_flat(rows_out, kap, half, j).astype(BF16)
        return carry

    lax.fori_loop(0, own, keep, 0)
    apl[own * kap] = jnp.zeros(apl.shape[1:], BF16)
    apr[own * kap] = jnp.zeros(apr.shape[1:], BF16)

    reduce_plane(
        coarse_row, rows * per, (s1b, r1b, s2b, r2b, s1b_c, r1b_c, s2b_c, r2b_c), acc_b,
        (s1b_send, s1b_recv, s2b_send, s2b_recv),
    )
    third = []
    for d in list(range(1, rows)) + [0]:
        to = lax.rem(row + d, rows)
        for q in range(per):
            value = acc_b[to * per + q]
            if d:
                s3[d - 1, q], s3_c[d - 1, pl.ds(q, 1), :] = pack(value)
            else:
                mine_b[q] = value
        if d:
            for w, (src, dst) in enumerate(((s3, r3), (s3_c, r3_c))):
                copy = pltpu.make_async_remote_copy(
                    src_ref=src.at[d - 1], dst_ref=dst.at[d - 1],
                    send_sem=s3_send.at[w, d - 1], recv_sem=s3_recv.at[w, d - 1],
                    device_id=(to, col), device_id_type=MESH,
                )
                copy.start()
                third.append(copy)
    for copy in third:
        copy.wait()
    for q in range(per):
        value = mine_b[q]
        for d in range(1, rows):
            value = value + unpack(r3[d - 1, q], r3_c[d - 1, pl.ds(q, 1), :])
        for t in range(0, kc, 2):
            x0, x1 = interleave(value[:, t * width : (t + 2) * width], left)
            rows_out[t * half : (t + 1) * half, :] = x0
            rows_out[(t + 1) * half : (t + 2) * half, :] = x1
        for j in range(half):
            coarse_out[q, :, j * 2 * width : (j + 1) * 2 * width] = to_flat(rows_out, kc, half, j)
    for h in range(rows - 1):
        done_send(*up(h))
        done_send(*down(h))


def shards(a_blocks, a_index, p_blocks, p_index, ap_index, coarse_index):
    rows, cols = lax.axis_size("row"), lax.axis_size("col")
    count, _, ka, flat = a_blocks.shape
    own, _, kp, _ = p_blocks.shape
    kap = ap_index.shape[1]
    coarse, kc = coarse_index.shape
    per = coarse // (rows * cols)
    width = int(round(flat ** 0.5))
    half = width // 2
    lanes = 2 * width

    groups = rows * own * kp
    across = -(-coarse // 128) * 128
    chips = cols // 2
    others = max(chips - 1, 1)
    wide = kap * width
    wide_c = kc * width
    vmem = pl.BlockSpec(memory_space=pltpu.VMEM)
    anywhere = pl.BlockSpec(memory_space=pl.ANY)
    dma = pltpu.SemaphoreType.DMA
    n_coarse = rows * per
    beyond = max(rows - 1, 1)

    def sums(n, across_lanes):
        pieces = pieces_of(n)
        depths = (2, chips * pieces, min(others * pieces, 6), others * pieces)
        return [
            *[pltpu.VMEM((k, n // pieces, width, across_lanes), LINK) for k in depths],
            *[pltpu.VMEM((k, n // pieces, across_lanes), F32) for k in depths],
            pltpu.VMEM((n, width, across_lanes), F32),
        ]

    def signals(n):
        pieces = pieces_of(n)
        return [dma((2, k * pieces)) for k in (chips, chips, others, others)]

    ap, coarse_out = pl.pallas_call(
        functools.partial(kernel, (rows, cols, own, ka, kp, kap, kc, per, groups)),
        out_shape=(
            jax.ShapeDtypeStruct((own, 1, kap, flat), BF16),
            jax.ShapeDtypeStruct((per, kc, flat), F32),
        ),
        in_specs=[vmem, vmem, anywhere, anywhere, anywhere, anywhere],
        out_specs=(vmem, vmem),
        scratch_shapes=[
            *[pltpu.SMEM(x.shape, jnp.int32) for x in (a_index, p_index, ap_index, coarse_index)],
            pltpu.VMEM((count, width, ka * width), BF16),
            pltpu.VMEM((rows, own * kp, half, lanes), BF16),
            pltpu.VMEM((rows * own, across), jnp.int32),
            pltpu.VMEM((own, across), jnp.int32),
            pltpu.VMEM((own, across), jnp.int32),
            pltpu.SMEM((rows * own, across), jnp.int32),
            pltpu.SMEM((own, across), jnp.int32),
            pltpu.SMEM((own, across), jnp.int32),
            pltpu.VMEM((2, max(ka, kp) * half, lanes), F32),
            pltpu.VMEM((max(kap, kc) * half, lanes), F32),
            pltpu.VMEM((groups + 1, width, lanes), BF16),
            pltpu.VMEM((groups + 1, width, lanes), BF16),
            pltpu.VMEM((own * kp + 1, width, lanes), BF16),
            pltpu.VMEM((own * kp + 1, width, lanes), BF16),
            pltpu.VMEM((own * kap + 1, width, lanes), BF16),
            pltpu.VMEM((own * kap + 1, width, lanes), BF16),
            *sums(own, wide),
            *sums(n_coarse, wide_c),
            pltpu.VMEM((per, width, wide_c), F32),
            pltpu.VMEM((beyond, per, width, wide_c), LINK),
            pltpu.VMEM((beyond, per, width, wide_c), LINK),
            pltpu.VMEM((beyond, per, wide_c), F32),
            pltpu.VMEM((beyond, per, wide_c), F32),
            dma((beyond,)), dma((beyond,)), dma((beyond,)), dma((beyond,)), dma((beyond,)), dma((beyond,)), dma((7,)),
            *signals(own), *signals(n_coarse),
            dma((2, beyond)), dma((2, beyond)),
        ],
        compiler_params=pltpu.CompilerParams(
            collective_id=0, has_side_effects=True, vmem_limit_bytes=60 * 1024 * 1024
        ),
    )(a_blocks, p_blocks, a_index, p_index, ap_index, coarse_index)
    return ap, coarse_out


def solution(mesh):
    placed = (
        P("row", "col", None, None),
        P("row", "col", None),
        P("row", "col", None, None),
        P("row", "col", None),
        P("row", None),
        P(),
    )
    return jax.shard_map(
        shards,
        mesh=mesh,
        in_specs=placed,
        out_specs=(P("row", "col", None, None), P(("row", "col"), None, None)),
        check_vma=False,
    )
```

```python
import functools

import jax
import jax.numpy as jnp
from jax import lax
from jax.experimental import pallas as pl
from jax.experimental.pallas import tpu as pltpu
from jax.sharding import PartitionSpec as P

MESH = pl.DeviceIdType.MESH
F32 = jnp.float32
BF16 = jnp.bfloat16
LINK = jnp.int16
TOP = 32766.0


def left_mask(half):
    return lax.broadcasted_iota(jnp.int32, (half, 4 * half), 1) < 2 * half


def swap(x):
    return pltpu.roll(x, x.shape[1] // 2, 1)


def halves(x, left):
    other = swap(x)
    zero = jnp.zeros_like(x)
    in_left = jnp.concatenate([jnp.where(left, x, zero), jnp.where(left, other, zero)], axis=0)
    in_right = jnp.concatenate([jnp.where(left, zero, other), jnp.where(left, zero, x)], axis=0)
    return in_left.astype(BF16), in_right.astype(BF16)


def interleave(tile, left):
    half = left.shape[0]
    top, bottom = tile[:half], tile[half:]
    return jnp.where(left, top, swap(bottom)), jnp.where(left, swap(top), bottom)


def pack(value):
    most = jnp.maximum(jnp.max(jnp.abs(value), axis=0, keepdims=True), 1e-30)
    return jnp.round(value * (TOP / most)).astype(jnp.int32).astype(LINK), most * (1.0 / TOP)


def unpack(value, scale):
    return value.astype(jnp.int32).astype(F32) * scale


def pieces_of(count):
    return 2 if count % 2 == 0 else 1


def gather_tiles(in_left, in_right, picks):
    return jnp.concatenate(
        [in_left[picks[n]] + in_right[picks[n + 1]] for n in range(0, len(picks), 2)], axis=1
    )


def turn_prolongator(left, own_ref, pt_l, pt_r, mine):
    half, lanes = left.shape
    into = lax.broadcasted_iota(jnp.int32, (2 * half, lanes), 0)
    source = lax.rem(into, half) * 2 + into // half
    order_mat = (source == lax.broadcasted_iota(jnp.int32, (2 * half, lanes), 1)).astype(F32).astype(BF16)
    contract = (((1,), (1,)), ((), ()))

    def body(n, carry):
        block = halves(own_ref[n].astype(F32), left)[0]
        zero = jnp.zeros_like(block)
        for ref, pair in ((pt_l, [block, zero]), (pt_r, [zero, block])):
            ref[n] = lax.dot_general(
                order_mat, jnp.concatenate(pair, axis=0), contract, preferred_element_type=F32
            ).astype(BF16)
        return carry

    lax.fori_loop(0, mine, body, 0, unroll=4)
    pt_l[mine] = jnp.zeros(pt_l.shape[1:], BF16)
    pt_r[mine] = jnp.zeros(pt_r.shape[1:], BF16)


def to_rows(flat, out, half):
    n, lanes = flat.shape[0], out.shape[1]
    for j in range(half):
        out[pl.ds(j, n, stride=half), :] = flat[:, j * lanes : (j + 1) * lanes]


def to_flat(rows_ref, n, half, j):
    return rows_ref[pl.ds(j, n, stride=half), :]


def kernel(
    sizes, a_ref, p_ref, fine_any, pcol_any, kept_any, cols_any,
    ap_out, coarse_out,
    fine_ref, pcol_ref, kept_ref, cols_ref, a_pre, pg, tables, local, spots, places, local_places, spot_places, rows_in, rows_out,
    pl_l, pl_r, pt_l, pt_r, apl, apr,
    s1a, r1a, s2a, r2a, s1a_c, r1a_c, s2a_c, r2a_c, acc_a,
    s1b, r1b, s2b, r2b, s1b_c, r1b_c, s2b_c, r2b_c, acc_b, mine_b, s3, r3, s3_c, r3_c,
    up_send, up_recv, down_send, down_recv, table_send, table_recv, place_sem,
    s1a_send, s1a_recv, s2a_send, s2a_recv, s1b_send, s1b_recv, s2b_send, s2b_recv, s3_send, s3_recv,
):
    rows, cols, own, ka, kp, kap, kc, per, groups = sizes
    chips = cols // 2
    half = pg.shape[2]
    width = 2 * half
    left = left_mask(half)
    row, col = lax.axis_index("row"), lax.axis_index("col")
    core = lax.rem(col, 2)
    chip = col // 2
    partner = chip * 2 + 1 - core

    barrier = pltpu.get_barrier_semaphore()
    pl.semaphore_signal(barrier, inc=1, device_id=(row, partner), device_id_type=MESH)
    for d in range(1, chips):
        there = lax.rem(chip + d, chips) * 2 + core
        pl.semaphore_signal(barrier, inc=1, device_id=(row, there), device_id_type=MESH)
    for d in range(1, rows):
        pl.semaphore_signal(
            barrier, inc=1, device_id=(lax.rem(row + d, rows), col), device_id_type=MESH
        )

    mine = own * kp
    indices = [
        pltpu.make_async_copy(src, dst, place_sem.at[3 + n])
        for n, (src, dst) in enumerate(
            ((fine_any, fine_ref), (pcol_any, pcol_ref), (kept_any, kept_ref), (cols_any, cols_ref))
        )
    ]
    for copy in indices:
        copy.start()

    def lay_out(u, carry):
        to_rows(p_ref[u, 0].astype(F32), rows_in.at[0], half)
        for m in range(kp):
            pg[row, u * kp + m] = rows_in[0, m * half : (m + 1) * half, :].astype(BF16)
        return carry

    lax.fori_loop(0, own, lay_out, 0)
    pl.semaphore_wait(barrier, chips + rows - 1)

    def up(h):
        shard = row - h
        return (shard >= 0) & (row + 1 < rows), pltpu.make_async_remote_copy(
            src_ref=pg.at[shard], dst_ref=pg.at[shard],
            send_sem=up_send.at[h], recv_sem=up_recv.at[h],
            device_id=(row + 1, col), device_id_type=MESH,
        )

    def down(h):
        shard = row + h
        return (shard < rows) & (row > 0), pltpu.make_async_remote_copy(
            src_ref=pg.at[shard], dst_ref=pg.at[shard],
            send_sem=down_send.at[h], recv_sem=down_recv.at[h],
            device_id=(row - 1, col), device_id_type=MESH,
        )

    def start(ready, copy):
        @pl.when(ready)
        def _():
            copy.start()

    def done_send(ready, copy):
        @pl.when(ready)
        def _():
            copy.wait_send()

    into = lax.broadcasted_iota(jnp.int32, (width, width), 0)
    natural = lax.rem(into, 2) * half + into // 2 == lax.broadcasted_iota(jnp.int32, (width, width), 1)
    natural = natural.astype(F32).astype(BF16)

    def spread(shard):
        def body(n, carry):
            pair = jnp.concatenate(halves(pg[shard, n].astype(F32), left), axis=1)
            pair = jnp.dot(natural, pair, preferred_element_type=F32).astype(BF16)
            pl_l[shard * mine + n] = pair[:, : 2 * width]
            pl_r[shard * mine + n] = pair[:, 2 * width :]
            return carry

        lax.fori_loop(0, mine, body, 0, unroll=4)

    start(*up(0))
    start(*down(0))
    for copy in indices:
        copy.wait()
    lane = lax.broadcasted_iota(jnp.int32, (1, tables.shape[1]), 1)
    lines = []
    for u in range(own):
        line = jnp.full(lane.shape, mine, jnp.int32)
        for m in range(kp):
            line = jnp.where(lane == pcol_ref[0, m, u], u * kp + m, line)
        lines.append(line)
        spot = jnp.full(lane.shape, own * kap, jnp.int32)
        for n in range(kap):
            spot = jnp.where(lane == kept_ref[n, u * cols + col], u * kap + n, spot)
        spots[u : u + 1, :] = spot
    lines = jnp.concatenate(lines, axis=0)
    local[...] = lines
    here = pl.ds(pl.multiple_of(row * own, own), own)
    tables[here, :] = jnp.where(lines < mine, lines + row * mine, groups)
    pl_l[groups] = jnp.zeros(pl_l.shape[1:], BF16)
    pl_r[groups] = jnp.zeros(pl_r.shape[1:], BF16)
    table_copies = []
    for d in range(1, rows):
        copy = pltpu.make_async_remote_copy(
            src_ref=tables.at[here], dst_ref=tables.at[here],
            send_sem=table_send.at[d - 1], recv_sem=table_recv.at[d - 1],
            device_id=(lax.rem(row + d, rows), col), device_id_type=MESH,
        )
        copy.start()
        table_copies.append(copy)
    small = [
        pltpu.make_async_copy(local, local_places, place_sem.at[0]),
        pltpu.make_async_copy(spots, spot_places, place_sem.at[1]),
    ]
    for copy in small:
        copy.start()

    def lay_rows(n, carry):
        for k in range(2):
            i = n * 2 + k
            to_rows(a_ref[i, 0].astype(F32), rows_in.at[k], half)
            for e in range(0, ka, 2):
                x0 = rows_in[k, e * half : (e + 1) * half, :]
                x1 = rows_in[k, (e + 1) * half : (e + 2) * half, :]
                top = jnp.where(left, x0, swap(x1))
                bottom = jnp.where(left, swap(x0), x1)
                tile = jnp.concatenate([top, bottom], axis=0).astype(BF16)
                a_pre[i, :, e * width : (e + 2) * width] = tile
        return carry

    lax.fori_loop(0, a_ref.shape[0] // 2, lay_rows, 0)
    spread(row)
    turn_prolongator(left, pg.at[row], pt_l, pt_r, mine)
    for copy in table_copies:
        copy.wait()
    small.append(pltpu.make_async_copy(tables, places, place_sem.at[2]))
    small[2].start()
    for h in range(rows - 1):
        @pl.when(row - 1 - h >= 0)
        def _():
            up(h)[1].wait_recv()

        if h + 1 < rows - 1:
            start(*up(h + 1))

        @pl.when(row + 1 + h < rows)
        def _():
            down(h)[1].wait_recv()

        if h + 1 < rows - 1:
            start(*down(h + 1))

        @pl.when(row - 1 - h >= 0)
        def _():
            spread(row - 1 - h)

        @pl.when(row + 1 + h < rows)
        def _():
            spread(row + 1 + h)

    for copy in small:
        copy.wait()

    def product_row(to, u):
        i = u * cols + to
        kept = [kept_ref[n, i] for n in range(kap)]
        fine = [fine_ref[0, e, i] for e in range(ka)]
        rhs = [gather_tiles(pl_l, pl_r, [places[k, j] for j in kept]) for k in fine]
        return jnp.dot(a_pre[i], jnp.concatenate(rhs, axis=0), preferred_element_type=F32)

    def coarse_row(to, n):
        j = ((n // per) * cols + to) * per + lax.rem(n, per)
        lhs = gather_tiles(pt_l, pt_r, [local_places[u, j] for u in range(own)])
        kept = [cols_ref[t, j] for t in range(kc)]
        rhs = [gather_tiles(apl, apr, [spot_places[u, c] for c in kept]) for u in range(own)]
        return jnp.dot(lhs, jnp.concatenate(rhs, axis=0), preferred_element_type=F32)

    nx = 2 if chips % 2 == 0 else 1
    ny = chips // nx
    chip_y, chip_x = chip // nx, lax.rem(chip, nx)

    def column(step, on):
        return (lax.rem(chip_y + step[0], ny) * nx + lax.rem(chip_x + step[1], nx)) * 2 + on

    def reduce_plane(compute, count, bufs, acc, sems):
        s1, r1, s2, r2, s1_c, r1_c, s2_c, r2_c = bufs
        s1_send, s1_recv, s2_send, s2_recv = sems
        pieces = pieces_of(count)
        size = count // pieces
        far = [(dy, 1) for dy in range(1, ny)] if nx == 2 else []
        along_x = [(0, 1)] if nx == 2 else []
        along_y = [(dy, 0) for dy in range(1, ny)]
        plan = []
        for leg in range(4):
            for p in range(pieces):
                x_first = p % 2 == 0
                if leg == 0:
                    plan += [(p, d, (0, 1) if x_first else (d[0], 0), []) for d in far]
                elif leg == 1:
                    plan += [(p, d, d, []) for d in (along_x if x_first else along_y)]
                elif leg == 2 and x_first:
                    plan += [(p, d, d, [(d[0], 1)] if far else []) for d in along_y]
                elif leg == 2:
                    plan += [(p, d, d, far) for d in along_x]
                else:
                    plan.append((p, (0, 0), None, along_x + along_y))
        first, second, place = [], [], {}

        def start(src, dst, slot, n, send, recv, device):
            copies = [
                pltpu.make_async_remote_copy(
                    src_ref=a.at[slot], dst_ref=b.at[n], send_sem=send.at[w, n], recv_sem=recv.at[w, n],
                    device_id=(row, device), device_id_type=MESH,
                )
                for w, (a, b) in enumerate(zip(src, dst))
            ]
            for copy in copies:
                copy.start()
            return copies

        def give(n):
            p, d = plan[n][:2]
            to = column(d, 1 - core)
            slot = n % s1.shape[0]
            if n >= s1.shape[0]:
                for copy in first[n - s1.shape[0]]:
                    copy.wait_send()

            def body(k, carry):
                s1[slot, k], s1_c[slot, pl.ds(k, 1), :] = pack(compute(to, p * size + k))
                return carry

            lax.fori_loop(0, size, body, 0, unroll=2)
            first.append(start((s1, s1_c), (r1, r1_c), slot, n, s1_send, s1_recv, partner))

        def arrived(p, adds):
            slots = [place[p, d] for d in adds]
            for m in slots:
                for copy in second[m]:
                    copy.wait_recv()
            return slots

        def finish(n):
            p, d, via, adds = plan[n]
            to = column(d, core)
            m = len(second)
            slot = m % s2.shape[0]
            for copy in first[n]:
                copy.wait_recv()
            slots = arrived(p, adds) if via else []
            if via and m >= s2.shape[0]:
                for copy in second[m - s2.shape[0]]:
                    copy.wait_send()

            def body(k, carry):
                value = compute(to, p * size + k) + unpack(r1[n, k], r1_c[n, pl.ds(k, 1), :])
                for other in slots:
                    value = value + unpack(r2[other, k], r2_c[other, pl.ds(k, 1), :])
                if via:
                    s2[slot, k], s2_c[slot, pl.ds(k, 1), :] = pack(value)
                else:
                    acc[p * size + k] = value
                return carry

            lax.fori_loop(0, size, body, 0, unroll=2)
            if via:
                place[p, d] = m
                second.append(start((s2, s2_c), (r2, r2_c), slot, m, s2_send, s2_recv, column(via, core)))

        for n in range(len(plan)):
            give(n)
            if n:
                finish(n - 1)
        finish(len(plan) - 1)
        for p, _, via, adds in plan:
            if via is None:
                slots = arrived(p, adds)

                def body(k, carry):
                    value = acc[p * size + k]
                    for other in slots:
                        value = value + unpack(r2[other, k], r2_c[other, pl.ds(k, 1), :])
                    acc[p * size + k] = value
                    return carry

                lax.fori_loop(0, size, body, 0, unroll=2)
        for copies in first[-s1.shape[0]:] + second[-s2.shape[0]:]:
            for copy in copies:
                copy.wait_send()

    reduce_plane(
        product_row, own, (s1a, r1a, s2a, r2a, s1a_c, r1a_c, s2a_c, r2a_c), acc_a,
        (s1a_send, s1a_recv, s2a_send, s2a_recv),
    )

    def keep(u, carry):
        value = acc_a[u].astype(BF16).astype(F32)
        for s in range(0, kap, 2):
            tile = value[:, s * width : (s + 2) * width]
            x0, x1 = interleave(tile, left)
            rows_out[s * half : (s + 1) * half, :] = x0
            rows_out[(s + 1) * half : (s + 2) * half, :] = x1
            for n, x in ((s, x0), (s + 1, x1)):
                in_left, in_right = halves(x, left)
                apl[u * kap + n] = in_left
                apr[u * kap + n] = in_right
        for j in range(half):
            ap_out[u, 0, :, j * 2 * width : (j + 1) * 2 * width] = to_flat(rows_out, kap, half, j).astype(BF16)
        return carry

    lax.fori_loop(0, own, keep, 0)
    apl[own * kap] = jnp.zeros(apl.shape[1:], BF16)
    apr[own * kap] = jnp.zeros(apr.shape[1:], BF16)

    reduce_plane(
        coarse_row, rows * per, (s1b, r1b, s2b, r2b, s1b_c, r1b_c, s2b_c, r2b_c), acc_b,
        (s1b_send, s1b_recv, s2b_send, s2b_recv),
    )
    third = []
    for d in list(range(1, rows)) + [0]:
        to = lax.rem(row + d, rows)
        for q in range(per):
            value = acc_b[to * per + q]
            if d:
                s3[d - 1, q], s3_c[d - 1, pl.ds(q, 1), :] = pack(value)
            else:
                mine_b[q] = value
        if d:
            for w, (src, dst) in enumerate(((s3, r3), (s3_c, r3_c))):
                copy = pltpu.make_async_remote_copy(
                    src_ref=src.at[d - 1], dst_ref=dst.at[d - 1],
                    send_sem=s3_send.at[w, d - 1], recv_sem=s3_recv.at[w, d - 1],
                    device_id=(to, col), device_id_type=MESH,
                )
                copy.start()
                third.append(copy)
    for copy in third:
        copy.wait()
    for q in range(per):
        value = mine_b[q]
        for d in range(1, rows):
            value = value + unpack(r3[d - 1, q], r3_c[d - 1, pl.ds(q, 1), :])
        for t in range(0, kc, 2):
            x0, x1 = interleave(value[:, t * width : (t + 2) * width], left)
            rows_out[t * half : (t + 1) * half, :] = x0
            rows_out[(t + 1) * half : (t + 2) * half, :] = x1
        for j in range(half):
            coarse_out[q, :, j * 2 * width : (j + 1) * 2 * width] = to_flat(rows_out, kc, half, j)
    for h in range(rows - 1):
        done_send(*up(h))
        done_send(*down(h))


def shards(a_blocks, a_index, p_blocks, p_index, ap_index, coarse_index):
    rows, cols = lax.axis_size("row"), lax.axis_size("col")
    count, _, ka, flat = a_blocks.shape
    own, _, kp, _ = p_blocks.shape
    kap = ap_index.shape[1]
    coarse, kc = coarse_index.shape
    per = coarse // (rows * cols)
    width = int(round(flat ** 0.5))
    half = width // 2
    lanes = 2 * width

    turned = (a_index.transpose(1, 2, 0), p_index.transpose(1, 2, 0), ap_index.T, coarse_index.T)
    groups = rows * own * kp
    across = -(-coarse // 128) * 128
    chips = cols // 2
    others = max(chips - 1, 1)
    wide = kap * width
    wide_c = kc * width
    vmem = pl.BlockSpec(memory_space=pltpu.VMEM)
    anywhere = pl.BlockSpec(memory_space=pl.ANY)
    dma = pltpu.SemaphoreType.DMA
    n_coarse = rows * per
    beyond = max(rows - 1, 1)

    def sums(n, across_lanes):
        pieces = pieces_of(n)
        depths = (2, chips * pieces, min(others * pieces, 6), others * pieces)
        return [
            *[pltpu.VMEM((k, n // pieces, width, across_lanes), LINK) for k in depths],
            *[pltpu.VMEM((k, n // pieces, across_lanes), F32) for k in depths],
            pltpu.VMEM((n, width, across_lanes), F32),
        ]

    def signals(n):
        pieces = pieces_of(n)
        return [dma((2, k * pieces)) for k in (chips, chips, others, others)]

    ap, coarse_out = pl.pallas_call(
        functools.partial(kernel, (rows, cols, own, ka, kp, kap, kc, per, groups)),
        out_shape=(
            jax.ShapeDtypeStruct((own, 1, kap, flat), BF16),
            jax.ShapeDtypeStruct((per, kc, flat), F32),
        ),
        in_specs=[vmem, vmem, anywhere, anywhere, anywhere, anywhere],
        out_specs=(vmem, vmem),
        scratch_shapes=[
            *[pltpu.SMEM(x.shape, jnp.int32) for x in turned],
            pltpu.VMEM((count, width, ka * width), BF16),
            pltpu.VMEM((rows, own * kp, half, lanes), BF16),
            pltpu.VMEM((rows * own, across), jnp.int32),
            pltpu.VMEM((own, across), jnp.int32),
            pltpu.VMEM((own, across), jnp.int32),
            pltpu.SMEM((rows * own, across), jnp.int32),
            pltpu.SMEM((own, across), jnp.int32),
            pltpu.SMEM((own, across), jnp.int32),
            pltpu.VMEM((2, max(ka, kp) * half, lanes), F32),
            pltpu.VMEM((max(kap, kc) * half, lanes), F32),
            pltpu.VMEM((groups + 1, width, lanes), BF16),
            pltpu.VMEM((groups + 1, width, lanes), BF16),
            pltpu.VMEM((own * kp + 1, width, lanes), BF16),
            pltpu.VMEM((own * kp + 1, width, lanes), BF16),
            pltpu.VMEM((own * kap + 1, width, lanes), BF16),
            pltpu.VMEM((own * kap + 1, width, lanes), BF16),
            *sums(own, wide),
            *sums(n_coarse, wide_c),
            pltpu.VMEM((per, width, wide_c), F32),
            pltpu.VMEM((beyond, per, width, wide_c), LINK),
            pltpu.VMEM((beyond, per, width, wide_c), LINK),
            pltpu.VMEM((beyond, per, wide_c), F32),
            pltpu.VMEM((beyond, per, wide_c), F32),
            dma((beyond,)), dma((beyond,)), dma((beyond,)), dma((beyond,)), dma((beyond,)), dma((beyond,)), dma((7,)),
            *signals(own), *signals(n_coarse),
            dma((2, beyond)), dma((2, beyond)),
        ],
        compiler_params=pltpu.CompilerParams(
            collective_id=0, has_side_effects=True, vmem_limit_bytes=60 * 1024 * 1024
        ),
    )(a_blocks, p_blocks, *turned)
    return ap, coarse_out


def solution(mesh):
    placed = (
        P("row", "col", None, None),
        P("row", "col", None),
        P("row", "col", None, None),
        P("row", "col", None),
        P("row", None),
        P(),
    )
    return jax.shard_map(
        shards,
        mesh=mesh,
        in_specs=placed,
        out_specs=(P("row", "col", None, None), P(("row", "col"), None, None)),
        check_vma=False,
    )
```
